512 devices in a mesh: grp: 8 (over z), seq: 64 (over y, x, core).
Axes of the slice: x: 4, y: 8, z: 8, core: 2. Of those that a mesh axis runs over, the one named last changes fastest.
Arguments:
- rows: bfloat16 [8, 4096, 3, 4096], P('grp', 'seq'), may hold values from -6 to 6
- lengths: int32 [8], P('grp'), may hold values from 512 to 4096, as said below
- short_weight: float32 [3, 3, 4096], replicated, may hold values from -3 to 3
- long_filter: float32 [4096, 4096], P('seq', 'grp')
- filter_bias: float32 [4096], P('seq'), may hold values from -4 to 4
Outputs:
- mixed: bfloat16 [8, 4096, 4096], P('grp', 'seq')
The draws below stay inside these ranges and needn't reach their ends.
Inputs may be any that keep to these rules, and one draw needn't show every extreme that they name: `lengths`: in every draw some sequence has length 4096.
All inputs are finite; a program needn't handle non-finite values.
Results may differ from the reference program's by a relative error of at most 0.0057.
Values may be sent and summed in bfloat16 or wider, within the bound.
No kernel may reach another device: no remote copies, remote signals or barrier semaphores. Data moves between devices by JAX's collectives and lax.ppermute only.
A program may use at most 64 MiB of HBM per device.

```python
import math
import jax
import jax.numpy as jnp
from jax import lax

D = 4096
SEQS = 8
LEN = 4096


def draw_lengths(key, part):
    key = jax.random.fold_in(key, 5)
    first, second = jax.random.split(key)
    spread = jax.random.randint(first, (SEQS,), LEN // 8, LEN)
    chosen = jax.random.randint(second, (), 0, SEQS)
    return jnp.where(jnp.arange(SEQS, dtype=jnp.int32) == chosen, LEN, spread).astype(jnp.int32)


def draw_long_filter(key, part):
    first, second = jax.random.split(jax.random.fold_in(key, 17))
    lower = math.log(0.05 / LEN)
    upper = math.log(1.0 / 30.0)
    rate = jnp.exp(jax.random.uniform(first, (D, 1), jnp.float32, lower, upper))
    steps = jnp.arange(LEN, dtype=jnp.float32)[None, :]
    noise = jax.random.normal(second, (D, LEN), jnp.float32)
    scale = jnp.sqrt(2.0 * rate / (1.0 - jnp.exp(-2.0 * rate * LEN)))
    return (noise * jnp.exp(-rate * steps) * scale).astype(jnp.float32)


def block_scale(stream_key, dims, cuts, low, top_value):
    gain, own = 1.0, jax.random.fold_in(stream_key, 6)
    for axis_at, parts in cuts:
        heights = jnp.exp(jax.random.uniform(jax.random.fold_in(own, axis_at), (parts,), jnp.float32, low / len(cuts), top_value / len(cuts)))
        gain = gain * jnp.repeat(heights, dims[axis_at] // parts).reshape([-1 if axis == axis_at else 1 for axis in range(len(dims))])
    return gain


def normal_values(stream_key, extent, deviation, reach, cuts=(), kind=jnp.bfloat16):
    drawn = jax.random.normal(stream_key, extent, jnp.float32) * deviation
    if len(cuts) > 0:
        drawn = block_scale(stream_key, extent, cuts, -0.22, 0.18) * drawn
    return jnp.clip(drawn, min=-reach, max=reach).astype(kind)


def setup_inputs(seed: int = 0) -> dict:
    splits = jax.random.split(jax.random.key(seed), 6)
    return {
        "rows": normal_values(splits[0], (SEQS, LEN, 3, D), 1.0, 6.0, ((0, 8), (1, 64))),
        "lengths": draw_lengths(jax.random.fold_in(splits[5], 71), 0),
        "short_weight": normal_values(splits[2], (3, 3, D), 0.6, 3.0, (), jnp.float32),
        "long_filter": draw_long_filter(jax.random.fold_in(splits[5], 71), 0),
        "filter_bias": normal_values(splits[4], (D,), 1.0, 4.0, ((0, 64),), jnp.float32),
    }


def reference(rows, lengths, short_weight, long_filter, filter_bias):
    spectrum = jnp.fft.rfft(long_filter, n=2 * LEN, axis=1).T

    def one_sequence(args):
        x_rows, length = args
        live = (jnp.arange(LEN, dtype=jnp.int32) < length).astype(jnp.float32)
        masked = x_rows.astype(jnp.float32) * live[:, None, None]
        padded = jnp.concatenate([jnp.zeros((2, 3, D), jnp.float32), masked], 0)
        short = (short_weight[:, 0, :] * padded[2:] + short_weight[:, 1, :] * padded[1:-1]
                 + short_weight[:, 2, :] * padded[:-2])
        gated = lax.optimization_barrier((short[:, 1] * short[:, 2]).astype(jnp.bfloat16)).astype(jnp.float32)
        freq = jnp.fft.rfft(gated, n=2 * LEN, axis=0)
        conv = jnp.fft.irfft(freq * spectrum, n=2 * LEN, axis=0)[:LEN]
        output = conv + filter_bias[None, :] * gated
        output = lax.optimization_barrier(output.astype(jnp.bfloat16)).astype(jnp.float32)
        return (short[:, 0] * output * live[:, None]).astype(jnp.bfloat16)

    return lax.map(one_sequence, (rows, lengths))
```

```python
import math

import jax
import jax.numpy as jnp
import numpy as np
from jax import lax
from jax.experimental import pallas as pl
from jax.experimental.pallas import tpu as pltpu
from jax.sharding import PartitionSpec as P

BF16 = jnp.bfloat16
F32 = jnp.float32
VMEM_BYTES = 48 * 1024 * 1024


def split_hi_lo(table):
    high = table.astype(jnp.bfloat16)
    low = (table - high.astype(np.float64)).astype(jnp.bfloat16)
    return np.concatenate([high, low], axis=1)


def transform_tables(na, nb):
    n = na * nb
    a = np.arange(na)
    b = np.arange(nb)
    k1 = np.arange(na)
    angle = 2.0 * math.pi * np.outer(k1 + 0.25, a) / na
    first = np.concatenate([np.cos(angle), -np.sin(angle)], axis=0)
    order = np.concatenate([k1[0::2], k1[1::2]])
    back = 2.0 * math.pi * np.outer(a, order + 0.25) / na
    first_back = np.concatenate([np.cos(back), -np.sin(back)], axis=1)
    inner = 2.0 * math.pi * np.outer(b, b) / nb
    cos, sin = np.cos(inner), np.sin(inner)
    second = np.block([[cos, sin], [-sin, cos]])
    second_back = np.block([[cos, -sin], [sin, cos]])
    turn = 2.0 * math.pi * (k1[:, None] + 0.25) * b[None, :] / n
    turn = turn.reshape(na // 2, 2, nb).transpose(0, 2, 1)
    turn = np.repeat(turn, 64, axis=2)
    return (
        split_hi_lo(first),
        split_hi_lo(second),
        split_hi_lo(second_back),
        split_hi_lo(first_back),
        np.cos(turn).astype(np.float32),
        (-np.sin(turn)).astype(np.float32),
    )


def swap_halves(x):
    return pltpu.roll(x, 64, axis=1)


def lane_mix(one, two):
    low = lax.broadcasted_iota(jnp.int32, one.shape, 1) < 64
    return (
        jnp.where(low, one, swap_halves(two)),
        jnp.where(low, swap_halves(one), two),
    )


def twice(x):
    return jnp.concatenate([x, x], axis=0)


def dot(table, x):
    return jnp.dot(table, x, preferred_element_type=F32)


def block_stage(data32, mid, first, na, nr):
    for r in range(0, nr, 2):
        one = data32[pl.ds(r, na, stride=nr), :]
        two = data32[pl.ds(r + 1, na, stride=nr), :]
        both = jnp.concatenate([one, two], axis=1).astype(BF16)
        got = dot(first, twice(both))
        mid[pl.ds(r * 2 * na, 2 * na), :] = got[:, :128]
        mid[pl.ds((r + 1) * 2 * na, 2 * na), :] = got[:, 128:]


def turned(mid, turn_re, turn_im, p, na, nr):
    parts = []
    for ri in range(2):
        one = mid[pl.ds(ri * na + 2 * p, nr, stride=2 * na), :]
        two = mid[pl.ds(ri * na + 2 * p + 1, nr, stride=2 * na), :]
        top, bottom = lane_mix(one, two)
        parts.append(jnp.concatenate([top, bottom], axis=0))
    re, im = parts
    tre, tim = turn_re[p], turn_im[p]
    return re * tre - im * tim, re * tim + im * tre


def filter_kernel(filt, first, second, turn_re, turn_im, spec, data32, mid):
    na, nr, _ = filt.shape
    nb = 2 * nr
    data32[...] = filt[...].astype(F32).reshape(na * nr, 128)
    first, second = first[...], second[...]
    block_stage(data32, mid, first, na, nr)
    for p in range(0, na // 2, 2):
        cols = []
        for q in (p, p + 1):
            re, im = turned(mid, turn_re, turn_im, q, na, nr)
            cols.append(jnp.concatenate([re, im], axis=0))
        both = jnp.concatenate(cols, axis=1)
        high = both.astype(BF16)
        low = (both - high.astype(F32)).astype(BF16)
        got = dot(second, twice(high)) + dot(second[:, : 2 * nb], low)
        got = got * (1.0 / (na * nb))
        spec[p] = got[:, :128]
        spec[p + 1] = got[:, 128:]


def conv_kernel(z, spec, bias, first, second, second_back, first_back, turn_re, turn_im, out, data32, mid, mid_back):
    na, nr, _ = z.shape
    nb = 2 * nr
    data32[...] = z[...].astype(F32).reshape(na * nr, 128)
    first, second, second_back, first_back = first[...], second[...], second_back[...], first_back[...]
    block_stage(data32, mid, first, na, nr)
    for p in range(0, na // 2, 2):
        cols = []
        for q in (p, p + 1):
            re, im = turned(mid, turn_re, turn_im, q, na, nr)
            cols.append(jnp.concatenate([re, im], axis=0))
        got = dot(second, twice(jnp.concatenate(cols, axis=1).astype(BF16)))
        cols = []
        for j, q in enumerate((p, p + 1)):
            re, im = got[:nb, j * 128 : (j + 1) * 128], got[nb:, j * 128 : (j + 1) * 128]
            sre, sim = spec[q, pl.ds(0, nb), :], spec[q, pl.ds(nb, nb), :]
            cols.append(jnp.concatenate([re * sre - im * sim, re * sim + im * sre], axis=0))
        got = dot(second_back, twice(jnp.concatenate(cols, axis=1).astype(BF16)))
        for j, q in enumerate((p, p + 1)):
            re, im = got[:nb, j * 128 : (j + 1) * 128], got[nb:, j * 128 : (j + 1) * 128]
            tre, tim = turn_re[q], turn_im[q]
            mid_back[pl.ds(q * 2 * nb, nb), :] = re * tre + im * tim
            mid_back[pl.ds(q * 2 * nb + nb, nb), :] = im * tre - re * tim
    gain = bias[...]
    for r in range(0, nr, 2):
        cols = []
        for s in (r, r + 1):
            parts = []
            for ri in range(2):
                one = mid_back[pl.ds(ri * nb + s, na // 2, stride=2 * nb), :]
                two = mid_back[pl.ds(ri * nb + s + nr, na // 2, stride=2 * nb), :]
                parts.extend(lane_mix(one, two))
            cols.append(jnp.concatenate(parts, axis=0))
        got = dot(first_back, twice(jnp.concatenate(cols, axis=1).astype(BF16)))
        for j, s in enumerate((r, r + 1)):
            at = pl.ds(s, na, stride=nr)
            data32[at, :] = got[:, j * 128 : (j + 1) * 128] + gain * data32[at, :]
    out[...] = data32[...].reshape(na, nr, 128).astype(BF16)


def turn_filter_kernel(filt, out):
    for i in range(out.shape[0] // 2):
        block = filt[:, i * 128 : (i + 1) * 128].T
        for j in range(2):
            part = block[j * 64 : (j + 1) * 64]
            out[2 * i + j] = jnp.concatenate([part[:32], part[32:]], axis=1).astype(BF16)


def short_sum(x, halo, weights, alive):
    tok, width = x.shape
    row = lax.broadcasted_iota(jnp.int32, (tok, width), 0)
    x = jnp.where(row < alive, x.astype(F32), 0.0)
    halo = halo.astype(F32)
    before2 = jnp.where(alive > -2, halo[0:1], 0.0)
    before1 = jnp.where(alive > -1, halo[1:2], 0.0)
    back1 = jnp.where(row == 0, before1, pltpu.roll(x, 1, axis=0))
    back2 = jnp.where(row == 0, before2, jnp.where(row == 1, before1, pltpu.roll(x, 2, axis=0)))
    return weights[0:1] * x + weights[1:2] * back1 + weights[2:3] * back2


def gate_kernel(alive, rows, halo, weights, out):
    for i in range(rows.shape[2] // 128):
        at = pl.ds(i * 128, 128)
        key = short_sum(rows[0, :, at], halo[0, :, at], weights[0, :, at], alive[0])
        val = short_sum(rows[1, :, at], halo[1, :, at], weights[1, :, at], alive[0])
        z = key * val
        half = z.shape[0] // 2
        one, two = lane_mix(z[:half], z[half:])
        out[2 * i] = one.astype(BF16)
        out[2 * i + 1] = two.astype(BF16)


def query_kernel(alive, rows, halo, weights, out):
    for i in range(rows.shape[2] // 128):
        at = pl.ds(i * 128, 128)
        query = short_sum(rows[0, :, at], halo[0, :, at], weights[0, :, at], alive[0])
        row = lax.broadcasted_iota(jnp.int32, query.shape, 0)
        out[:, at] = jnp.where(row < alive[0], query, 0.0)


def mix_kernel(y, query, out):
    for i in range(out.shape[1] // 128):
        at = pl.ds(i * 128, 128)
        top, bottom = lane_mix(y[2 * i].astype(F32), y[2 * i + 1].astype(F32))
        out[:, at] = (query[:, at] * jnp.concatenate([top, bottom], axis=0)).astype(BF16)


def vmem(count):
    return [pl.BlockSpec(memory_space=pltpu.VMEM)] * count


def params():
    return pltpu.CompilerParams(vmem_limit_bytes=VMEM_BYTES)


def per_device(rows, lengths, short_weight, long_filter, filter_bias):
    tok, width = rows.shape[1], rows.shape[3]
    nseq = lax.axis_size("seq")
    ngrp = lax.axis_size("grp")
    me = lax.axis_index("seq")
    chans = width // nseq
    half = tok // 2
    span = long_filter.shape[1]
    parts = jnp.transpose(rows[0], (1, 0, 2))
    alive = lengths - me * tok
    halo = lax.ppermute(parts[:, tok - 2 :, :], "seq", [(i, i + 1) for i in range(nseq - 1)])
    tables = [jnp.asarray(t) for t in transform_tables(nseq, tok)]
    first, second, second_back, first_back, turn_re, turn_im = tables

    own = pl.pallas_call(
        turn_filter_kernel,
        out_shape=jax.ShapeDtypeStruct((span // tok, half, 2 * chans), BF16),
        in_specs=vmem(1),
        out_specs=pl.BlockSpec(memory_space=pltpu.VMEM),
        compiler_params=params(),
        name="turn_filter",
    )(long_filter)
    whole = lax.all_gather(own, "grp", axis=0, tiled=True)

    block = 1024
    z = pl.pallas_call(
        gate_kernel,
        grid=(width // block,),
        out_shape=jax.ShapeDtypeStruct((nseq, half, 2 * chans), BF16),
        in_specs=[
            pl.BlockSpec(memory_space=pltpu.SMEM),
            pl.BlockSpec((2, tok, block), lambda i: (0, 0, i)),
            pl.BlockSpec((2, 2, block), lambda i: (0, 0, i)),
            pl.BlockSpec((2, 3, block), lambda i: (0, 0, i)),
        ],
        out_specs=pl.BlockSpec((block // chans, half, 2 * chans), lambda i: (i, 0, 0)),
        compiler_params=params(),
        name="gate",
    )(alive, parts[1:], halo[1:], short_weight[1:])
    z = lax.all_to_all(z, "seq", split_axis=0, concat_axis=0, tiled=True)

    query = pl.pallas_call(
        query_kernel,
        grid=(width // block,),
        out_shape=jax.ShapeDtypeStruct((tok, width), F32),
        in_specs=[
            pl.BlockSpec(memory_space=pltpu.SMEM),
            pl.BlockSpec((1, tok, block), lambda i: (0, 0, i)),
            pl.BlockSpec((1, 2, block), lambda i: (0, 0, i)),
            pl.BlockSpec((1, 3, block), lambda i: (0, 0, i)),
        ],
        out_specs=pl.BlockSpec((tok, block), lambda i: (0, i)),
        compiler_params=params(),
        cost_estimate=pl.CostEstimate(flops=2000000, bytes_accessed=2000000, transcendentals=0),
        name="query",
    )(alive, parts, halo, short_weight)

    spec = pl.pallas_call(
        filter_kernel,
        out_shape=jax.ShapeDtypeStruct((nseq // 2, 2 * tok, 2 * chans), F32),
        in_specs=vmem(5),
        out_specs=pl.BlockSpec(memory_space=pltpu.VMEM),
        scratch_shapes=[
            pltpu.VMEM((nseq * half, 128), F32),
            pltpu.VMEM((half * 2 * nseq, 128), F32),
        ],
        compiler_params=params(),
        cost_estimate=pl.CostEstimate(flops=2000000000, bytes_accessed=6000000, transcendentals=0),
        name="filter_spectrum",
    )(whole, first, second, turn_re, turn_im)

    bias = jnp.tile(filter_bias, 2)[None]
    y = pl.pallas_call(
        conv_kernel,
        out_shape=jax.ShapeDtypeStruct((nseq, half, 2 * chans), BF16),
        in_specs=vmem(9),
        out_specs=pl.BlockSpec(memory_space=pltpu.VMEM),
        scratch_shapes=[
            pltpu.VMEM((nseq * half, 128), F32),
            pltpu.VMEM((half * 2 * nseq, 128), F32),
            pltpu.VMEM((nseq * tok, 128), F32),
        ],
        compiler_params=params(),
        name="convolve",
    )(z, spec, bias, first, second, second_back, first_back, turn_re, turn_im)
    y = lax.all_to_all(y, "seq", split_axis=0, concat_axis=0, tiled=True)

    block = 1024
    out = pl.pallas_call(
        mix_kernel,
        grid=(width // block,),
        out_shape=jax.ShapeDtypeStruct((tok, width), BF16),
        in_specs=[
            pl.BlockSpec((block // chans, half, 2 * chans), lambda i: (i, 0, 0)),
            pl.BlockSpec((tok, block), lambda i: (0, i)),
        ],
        out_specs=pl.BlockSpec((tok, block), lambda i: (0, i)),
        compiler_params=params(),
        name="mix",
    )(y, query)
    return out[None]


def solution(mesh):
    in_specs = (P("grp", "seq", None, None), P("grp"), P(), P("seq", "grp"), P("seq"))
    out_specs = P("grp", "seq", None)
    return jax.shard_map(
        per_device, mesh=mesh, in_specs=in_specs, out_specs=out_specs, check_vma=False
    )
```

```python
import math

import jax
import jax.numpy as jnp
import numpy as np
from jax import lax
from jax.experimental import pallas as pl
from jax.experimental.pallas import tpu as pltpu
from jax.sharding import PartitionSpec as P

BF16 = jnp.bfloat16
F32 = jnp.float32
FINE = 4
PAD = 4


def split_hi_lo(table):
    high = table.astype(jnp.bfloat16)
    low = (table - high.astype(np.float64)).astype(jnp.bfloat16)
    return np.concatenate([high, low], axis=1)


def transform_tables(na, nb):
    n = na * nb
    a = np.arange(na)
    b = np.arange(nb)
    k1 = np.arange(na)
    angle = 2.0 * math.pi * np.outer(k1 + 0.25, a) / na
    first = np.concatenate([np.cos(angle), -np.sin(angle)], axis=0)
    order = np.concatenate([k1[0::2], k1[1::2]])
    back = 2.0 * math.pi * np.outer(a, order + 0.25) / na
    first_back = np.concatenate([np.cos(back), -np.sin(back)], axis=1)
    inner = 2.0 * math.pi * np.outer(b, b) / nb
    cos, sin = np.cos(inner), np.sin(inner)
    second = np.block([[cos, sin], [-sin, cos]])
    second_back = np.block([[cos, -sin], [sin, cos]])
    turn = 2.0 * math.pi * (k1[:, None] + 0.25) * b[None, :] / n
    turn = turn.reshape(na // 2, 2, nb).transpose(0, 2, 1)
    turn = np.repeat(turn, 64, axis=2)
    mats = [first, second, second_back, first_back]
    mats = [split_hi_lo(m) for m in mats]
    mats = [np.pad(m, ((0, 0), (0, 4 * nb - m.shape[1]))) for m in mats]
    factors = np.concatenate([turn[::FINE], turn[:FINE] - turn[:1]], axis=0)
    turns = np.stack([np.cos(factors), -np.sin(factors)]).astype(np.float32)
    return np.concatenate(mats, axis=0), turns


def swap_halves(x):
    return pltpu.roll(x, 64, axis=1)


def lane_mix(one, two):
    low = lax.broadcasted_iota(jnp.int32, one.shape, 1) < 64
    return (
        jnp.where(low, one, swap_halves(two)),
        jnp.where(low, swap_halves(one), two),
    )


def twice(x):
    return jnp.concatenate([x, x], axis=0)


def dot(table, x):
    return jnp.dot(table, x, preferred_element_type=F32)


def spread(data, data32):
    na, nr, _ = data.shape
    for a in range(na):
        data32[pl.ds(a * (nr + PAD), nr), :] = data[a].astype(F32)


def block_stage(data32, mid, first, na, nr):
    for r in range(0, nr, 2):
        one = data32[pl.ds(r, na, stride=nr + PAD), :]
        two = data32[pl.ds(r + 1, na, stride=nr + PAD), :]
        both = jnp.concatenate([one, two], axis=1).astype(BF16)
        got = dot(first, twice(both))
        mid[pl.ds(r * (2 * na + PAD), 2 * na), :] = got[:, :128]
        mid[pl.ds((r + 1) * (2 * na + PAD), 2 * na), :] = got[:, 128:]


def turn_of(turns, p):
    coarse = turns.shape[1] - FINE
    are, aim = turns[0, p // FINE], turns[1, p // FINE]
    if p % FINE == 0:
        return are, aim
    bre, bim = turns[0, coarse + p % FINE], turns[1, coarse + p % FINE]
    return are * bre - aim * bim, are * bim + aim * bre


def turned(mid, turn, p, na, nr):
    parts = []
    for ri in range(2):
        one = mid[pl.ds(ri * na + 2 * p, nr, stride=2 * na + PAD), :]
        two = mid[pl.ds(ri * na + 2 * p + 1, nr, stride=2 * na + PAD), :]
        top, bottom = lane_mix(one, two)
        parts.append(jnp.concatenate([top, bottom], axis=0))
    re, im = parts
    tre, tim = turn
    return re * tre - im * tim, re * tim + im * tre


def copies(pairs, sems):
    made = [pltpu.make_async_copy(src, dst, sems.at[i]) for i, (src, dst) in enumerate(pairs)]
    for copy in made:
        copy.start()
    return made


def spec_parts(spec_in, spec, step):
    parts = [pl.ds(i, step) for i in range(0, spec.shape[0], step)]
    return [(spec_in.at[part], spec.at[part]) for part in parts]


def filter_kernel(place, own, across, one_on, one_back, bias, mats_in, turns_in, spec_out, data32, mid, spec, mats, turns, sems):
    na, nr = 4 * own.shape[0], own.shape[1]
    nb = 2 * nr
    step = na // 8
    made = copies([(mats_in, mats), (turns_in, turns)], sems)
    shards = 8
    rows = na // shards
    turned_round = 2 + 4 * lax.rem(place[0], 2)
    for source, start in ((own, 0), (across, turned_round), (one_on, 1), (one_back, 7)):
        for j in range(2):
            shard = lax.rem(place[0] + start + 4 * j, shards)
            base = pl.multiple_of(shard * (rows * (nr + PAD)), 8)
            for i in range(rows):
                data32[pl.ds(base + i * (nr + PAD), nr), :] = source[j * rows + i].astype(F32)
    made[0].wait()
    first = mats[0 : 2 * na, 0 : 2 * na]
    second = mats[2 * na : 2 * na + 2 * nb, :]
    block_stage(data32, mid, first, na, nr)
    made[1].wait()
    leaving = []
    delta = bias[...]
    delta = jnp.concatenate([delta, delta], axis=1)
    for p in range(0, na // 2, 2):
        cols, turn = [], []
        for q in (p, p + 1):
            turn.append(turn_of(turns, q))
            re, im = turned(mid, turn[-1], q, na, nr)
            cols.append(jnp.concatenate([re, im], axis=0))
        both = jnp.concatenate(cols, axis=1)
        high = both.astype(BF16)
        low = (both - high.astype(F32)).astype(BF16)
        got = dot(second, twice(high)) + dot(second[:, : 2 * nb], low)
        scale = 1.0 / (na * nb)
        for j, q in enumerate((p, p + 1)):
            spec[q, pl.ds(0, nb), :] = ((got[:nb, j * 128 : (j + 1) * 128] + delta) * scale).astype(BF16)
            spec[q, pl.ds(nb, nb), :] = (got[nb:, j * 128 : (j + 1) * 128] * scale).astype(BF16)
        if (p + 2) % step == 0:
            part = pl.ds(p + 2 - step, step)
            leave = pltpu.make_async_copy(spec.at[part], spec_out.at[part], sems.at[2 + p // step])
            leave.start()
            leaving.append(leave)
    for leave in leaving:
        leave.wait()


def conv_kernel(z, spec_in, mats_in, turns_in, out, data32, mid, mid_back, spec, mats, turns, sems):
    na, nr, _ = z.shape
    nb = 2 * nr
    step = na // 8
    made = copies([(mats_in, mats), (turns_in, turns)] + spec_parts(spec_in, spec, step), sems)
    spread(z, data32)
    made[0].wait()
    at = 2 * na
    first = mats[0:at, 0 : 2 * na]
    second = mats[at : at + 2 * nb, :]
    second_back = mats[at + 2 * nb : at + 4 * nb, :]
    first_back = mats[at + 4 * nb :, :]
    block_stage(data32, mid, first, na, nr)
    for p in range(0, na // 2, 2):
        if p == 0:
            made[1].wait()
        if p % step == 0:
            made[2 + p // step].wait()
        cols, turn = [], []
        for q in (p, p + 1):
            turn.append(turn_of(turns, q))
            re, im = turned(mid, turn[-1], q, na, nr)
            cols.append(jnp.concatenate([re, im], axis=0))
        got = dot(second, twice(jnp.concatenate(cols, axis=1).astype(BF16)))
        cols = []
        for j, q in enumerate((p, p + 1)):
            re, im = got[:nb, j * 128 : (j + 1) * 128], got[nb:, j * 128 : (j + 1) * 128]
            sre, sim = spec[q, pl.ds(0, nb), :].astype(F32), spec[q, pl.ds(nb, nb), :].astype(F32)
            cols.append(jnp.concatenate([re * sre - im * sim, re * sim + im * sre], axis=0))
        got = dot(second_back, twice(jnp.concatenate(cols, axis=1).astype(BF16)))
        for j, q in enumerate((p, p + 1)):
            re, im = got[:nb, j * 128 : (j + 1) * 128], got[nb:, j * 128 : (j + 1) * 128]
            tre, tim = turn[j]
            mid_back[pl.ds(q * (2 * nb + PAD), nb), :] = re * tre + im * tim
            mid_back[pl.ds(q * (2 * nb + PAD) + nb, nb), :] = im * tre - re * tim
    for r in range(0, nr, 2):
        cols = []
        for s in (r, r + 1):
            parts = []
            for ri in range(2):
                one = mid_back[pl.ds(ri * nb + s, na // 2, stride=2 * nb + PAD), :]
                two = mid_back[pl.ds(ri * nb + s + nr, na // 2, stride=2 * nb + PAD), :]
                parts.extend(lane_mix(one.astype(BF16), two.astype(BF16)))
            cols.append(jnp.concatenate(parts, axis=0))
        got = dot(first_back, twice(jnp.concatenate(cols, axis=1)))
        for j, s in enumerate((r, r + 1)):
            data32[pl.ds(s, na, stride=nr + PAD), :] = got[:, j * 128 : (j + 1) * 128]
    for a in range(na):
        out[a] = data32[pl.ds(a * (nr + PAD), nr), :].astype(BF16)


def turn_filter_kernel(filt, out):
    for i in range(out.shape[0] // 2):
        block = filt[:, i * 128 : (i + 1) * 128].T
        for j in range(2):
            part = block[j * 64 : (j + 1) * 64]
            out[2 * i + j] = jnp.concatenate([part[:32], part[32:]], axis=1).astype(BF16)


def short_sum(x, halo, weights, alive):
    tok, width = x.shape
    row = lax.broadcasted_iota(jnp.int32, (tok, width), 0)
    x = jnp.where(row < alive, x.astype(F32), 0.0)
    halo = halo.astype(F32)
    before2 = jnp.where(alive > -2, halo[0:1], 0.0)
    before1 = jnp.where(alive > -1, halo[1:2], 0.0)
    back1 = jnp.where(row == 0, before1, pltpu.roll(x, 1, axis=0))
    back2 = jnp.where(row == 0, before2, jnp.where(row == 1, before1, pltpu.roll(x, 2, axis=0)))
    return weights[0:1] * x + weights[1:2] * back1 + weights[2:3] * back2


def gate_kernel(alive, rows, halo, weights, out):
    for i in range(rows.shape[2] // 128):
        at = pl.ds(i * 128, 128)
        key = short_sum(rows[0, :, at], halo[1, :, at], weights[0, :, at], alive[0])
        val = short_sum(rows[1, :, at], halo[2, :, at], weights[1, :, at], alive[0])
        z = key * val
        half = z.shape[0] // 2
        one, two = lane_mix(z[:half], z[half:])
        out[2 * i] = one.astype(BF16)
        out[2 * i + 1] = two.astype(BF16)


def query_kernel(alive, rows, halo, weights, out):
    for i in range(rows.shape[2] // 128):
        at = pl.ds(i * 128, 128)
        query = short_sum(rows[0, :, at], halo[0, :, at], weights[0, :, at], alive[0])
        row = lax.broadcasted_iota(jnp.int32, query.shape, 0)
        out[:, at] = jnp.where(row < alive[0], query, 0.0)


def mix_kernel(y, query, out):
    for i in range(out.shape[1] // 128):
        at = pl.ds(i * 128, 128)
        top, bottom = lane_mix(y[2 * i].astype(F32), y[2 * i + 1].astype(F32))
        out[:, at] = (query[:, at] * jnp.concatenate([top, bottom], axis=0)).astype(BF16)


def vmem(count):
    return [pl.BlockSpec(memory_space=pltpu.VMEM)] * count


def params(limit):
    return pltpu.CompilerParams(vmem_limit_bytes=limit * 1024 * 1024)


def per_device(rows, lengths, short_weight, long_filter, filter_bias):
    tok, width = rows.shape[1], rows.shape[3]
    nseq = lax.axis_size("seq")
    ngrp = lax.axis_size("grp")
    me = lax.axis_index("seq")
    chans = width // nseq
    half = tok // 2
    span = long_filter.shape[1]
    parts = jnp.transpose(rows[0], (1, 0, 2))
    alive = lengths - me * tok
    last, long_filter = lax.optimization_barrier((parts[:, tok - 2 :, :], long_filter))
    halo = lax.ppermute(last, "seq", [(i, i + 1) for i in range(nseq - 1)])
    mats, turns = [jnp.asarray(t) for t in transform_tables(nseq, tok)]

    own = pl.pallas_call(
        turn_filter_kernel,
        out_shape=jax.ShapeDtypeStruct((span // tok, half, 2 * chans), BF16),
        in_specs=vmem(1),
        out_specs=pl.BlockSpec(memory_space=pltpu.VMEM),
        compiler_params=params(24),
        name="turn_filter",
    )(long_filter)
    group = lax.axis_index("grp")

    def from_shift(x, shift):
        return lax.ppermute(x, "grp", [((i + shift) % ngrp, i) for i in range(ngrp)])

    two = jnp.concatenate([own, from_shift(own, 4)], axis=0)
    pair = parts[1:]
    block = 1024
    z = pl.pallas_call(
        gate_kernel,
        grid=(width // block,),
        out_shape=jax.ShapeDtypeStruct((nseq, half, 2 * chans), BF16),
        in_specs=[
            pl.BlockSpec(memory_space=pltpu.SMEM),
            pl.BlockSpec((2, tok, block), lambda i: (0, 0, i)),
            pl.BlockSpec((3, 2, block), lambda i: (0, 0, i)),
            pl.BlockSpec((2, 3, block), lambda i: (0, 0, i)),
        ],
        out_specs=pl.BlockSpec((block // chans, half, 2 * chans), lambda i: (i, 0, 0)),
        compiler_params=params(48),
        name="gate",
    )(alive, pair, halo, short_weight[1:])
    z, two = lax.optimization_barrier((z, two))
    across = [((i + (2 if i % 2 == 0 else 6)) % ngrp, i) for i in range(ngrp)]
    others = [lax.ppermute(two, "grp", across), from_shift(two, 1), from_shift(two, 7)]
    z = lax.all_to_all(z, "seq", split_axis=0, concat_axis=0, tiled=True)

    query = pl.pallas_call(
        query_kernel,
        grid=(width // block,),
        out_shape=jax.ShapeDtypeStruct((tok, width), F32),
        in_specs=[
            pl.BlockSpec(memory_space=pltpu.SMEM),
            pl.BlockSpec((1, tok, block), lambda i: (0, 0, i)),
            pl.BlockSpec((1, 2, block), lambda i: (0, 0, i)),
            pl.BlockSpec((1, 3, block), lambda i: (0, 0, i)),
        ],
        out_specs=pl.BlockSpec((tok, block), lambda i: (0, i)),
        compiler_params=params(48),
        cost_estimate=pl.CostEstimate(flops=2000000, bytes_accessed=2000000, transcendentals=0),
        name="query",
    )(alive, parts, halo, short_weight)

    hbm = pl.BlockSpec(memory_space=pltpu.HBM)
    table_scratch = [
        pltpu.VMEM((nseq // 2, 2 * tok, 2 * chans), BF16),
        pltpu.VMEM(mats.shape, BF16),
        pltpu.VMEM(turns.shape, F32),
    ]
    spec = pl.pallas_call(
        filter_kernel,
        out_shape=jax.ShapeDtypeStruct((nseq // 2, 2 * tok, 2 * chans), BF16),
        in_specs=[pl.BlockSpec(memory_space=pltpu.SMEM)] + vmem(5) + [hbm] * 2,
        out_specs=hbm,
        scratch_shapes=[
            pltpu.VMEM((nseq * (half + PAD), 128), F32),
            pltpu.VMEM((half * (2 * nseq + PAD), 128), F32),
            *table_scratch,
            pltpu.SemaphoreType.DMA((6,)),
        ],
        compiler_params=params(52),
        cost_estimate=pl.CostEstimate(flops=2000000000, bytes_accessed=6000000, transcendentals=0),
        name="filter_spectrum",
    )(group[None], two, *others, filter_bias[None], mats, turns)

    y = pl.pallas_call(
        conv_kernel,
        out_shape=jax.ShapeDtypeStruct((nseq, half, 2 * chans), BF16),
        in_specs=vmem(1) + [hbm] * 3,
        out_specs=pl.BlockSpec(memory_space=pltpu.VMEM),
        scratch_shapes=[
            pltpu.VMEM((nseq * (half + PAD), 128), F32),
            pltpu.VMEM((half * (2 * nseq + PAD), 128), F32),
            pltpu.VMEM((nseq // 2 * (2 * tok + PAD), 128), F32),
            *table_scratch,
            pltpu.SemaphoreType.DMA((6,)),
        ],
        compiler_params=params(52),
        name="convolve",
    )(z, spec, mats, turns)
    y = lax.all_to_all(y, "seq", split_axis=0, concat_axis=0, tiled=True)

    block = 1024
    out = pl.pallas_call(
        mix_kernel,
        grid=(width // block,),
        out_shape=jax.ShapeDtypeStruct((tok, width), BF16),
        in_specs=[
            pl.BlockSpec((block // chans, half, 2 * chans), lambda i: (i, 0, 0)),
            pl.BlockSpec((tok, block), lambda i: (0, i)),
        ],
        out_specs=pl.BlockSpec((tok, block), lambda i: (0, i)),
        compiler_params=params(24),
        name="mix",
    )(y, query)
    return out[None]


def solution(mesh):
    in_specs = (P("grp", "seq", None, None), P("grp"), P(), P("seq", "grp"), P("seq"))
    out_specs = P("grp", "seq", None)
    return jax.shard_map(
        per_device, mesh=mesh, in_specs=in_specs, out_specs=out_specs, check_vma=False
    )
```

```python
import math

import jax
import jax.numpy as jnp
import numpy as np
from jax import lax
from jax.experimental import pallas as pl
from jax.experimental.pallas import tpu as pltpu
from jax.sharding import PartitionSpec as P

BF16 = jnp.bfloat16
F32 = jnp.float32
FINE = 4
PAD = 4


def split_hi_lo(table):
    high = table.astype(jnp.bfloat16)
    low = (table - high.astype(np.float64)).astype(jnp.bfloat16)
    return np.concatenate([high, low], axis=1)


def transform_tables(na, nb):
    n = na * nb
    a = np.arange(na)
    b = np.arange(nb)
    k1 = np.arange(na)
    angle = 2.0 * math.pi * np.outer(k1 + 0.25, a) / na
    first = np.concatenate([np.cos(angle), -np.sin(angle)], axis=0)
    order = np.concatenate([k1[0::2], k1[1::2]])
    back = 2.0 * math.pi * np.outer(a, order + 0.25) / na
    first_back = np.concatenate([np.cos(back), -np.sin(back)], axis=1)
    inner = 2.0 * math.pi * np.outer(b, b) / nb
    cos, sin = np.cos(inner), np.sin(inner)
    second = np.block([[cos, sin], [-sin, cos]])
    second_back = np.block([[cos, -sin], [sin, cos]])
    turn = 2.0 * math.pi * (k1[:, None] + 0.25) * b[None, :] / n
    turn = turn.reshape(na // 2, 2, nb).transpose(0, 2, 1)
    turn = np.repeat(turn, 64, axis=2)
    mats = [first, second, second_back, first_back]
    mats = [split_hi_lo(m) for m in mats]
    mats = [np.pad(m, ((0, 0), (0, 4 * nb - m.shape[1]))) for m in mats]
    factors = np.concatenate([turn[::FINE], turn[:FINE] - turn[:1]], axis=0)
    turns = np.stack([np.cos(factors), -np.sin(factors)]).astype(np.float32)
    return np.concatenate(mats, axis=0), turns


def swap_halves(x):
    return pltpu.roll(x, 64, axis=1)


def lane_mix(one, two):
    low = lax.broadcasted_iota(jnp.int32, one.shape, 1) < 64
    return (
        jnp.where(low, one, swap_halves(two)),
        jnp.where(low, swap_halves(one), two),
    )


def twice(x):
    return jnp.concatenate([x, x], axis=0)


def dot(table, x):
    return jnp.dot(table, x, preferred_element_type=F32)


def spread(data, data32):
    na, nr, _ = data.shape
    for a in range(na):
        data32[pl.ds(a * (nr + PAD), nr), :] = data[a].astype(F32)


def block_stage(data32, mid, first, na, nr):
    for r in range(0, nr, 2):
        one = data32[pl.ds(r, na, stride=nr + PAD), :]
        two = data32[pl.ds(r + 1, na, stride=nr + PAD), :]
        both = jnp.concatenate([one, two], axis=1).astype(BF16)
        got = dot(first, twice(both))
        mid[pl.ds(r * (2 * na + PAD), 2 * na), :] = got[:, :128]
        mid[pl.ds((r + 1) * (2 * na + PAD), 2 * na), :] = got[:, 128:]


def turn_of(turns, p):
    coarse = turns.shape[1] - FINE
    are, aim = turns[0, p // FINE], turns[1, p // FINE]
    if p % FINE == 0:
        return are, aim
    bre, bim = turns[0, coarse + p % FINE], turns[1, coarse + p % FINE]
    return are * bre - aim * bim, are * bim + aim * bre


def turned(mid, turn, p, na, nr):
    parts = []
    for ri in range(2):
        one = mid[pl.ds(ri * na + 2 * p, nr, stride=2 * na + PAD), :]
        two = mid[pl.ds(ri * na + 2 * p + 1, nr, stride=2 * na + PAD), :]
        top, bottom = lane_mix(one, two)
        parts.append(jnp.concatenate([top, bottom], axis=0))
    re, im = parts
    tre, tim = turn
    return re * tre - im * tim, re * tim + im * tre


def copies(pairs, sems):
    made = [pltpu.make_async_copy(src, dst, sems.at[i]) for i, (src, dst) in enumerate(pairs)]
    for copy in made:
        copy.start()
    return made


def spec_parts(spec_in, spec, step):
    parts = [pl.ds(i, step) for i in range(0, spec.shape[0], step)]
    return [(spec_in.at[part], spec.at[part]) for part in parts]


def filter_kernel(place, own, across, one_on, one_back, bias, mats_in, turns_in, spec_out, data32, mid, spec, mats, turns, sems):
    na, nr = 4 * own.shape[0], own.shape[1]
    nb = 2 * nr
    step = na // 8
    made = copies([(mats_in, mats), (turns_in, turns)], sems)
    shards = 8
    rows = na // shards
    turned_round = 2 + 4 * lax.rem(place[0], 2)
    for source, start in ((own, 0), (across, turned_round), (one_on, 1), (one_back, 7)):
        for j in range(2):
            shard = lax.rem(place[0] + start + 4 * j, shards)
            base = pl.multiple_of(shard * (rows * (nr + PAD)), 8)
            for i in range(rows):
                data32[pl.ds(base + i * (nr + PAD), nr), :] = source[j * rows + i].astype(F32)
    made[0].wait()
    first = mats[0 : 2 * na, 0 : 2 * na]
    second = mats[2 * na : 2 * na + 2 * nb, :]
    block_stage(data32, mid, first, na, nr)
    made[1].wait()
    leaving = []
    delta = bias[...]
    delta = jnp.concatenate([delta, delta], axis=1)
    for p in range(0, na // 2, 2):
        cols, turn = [], []
        for q in (p, p + 1):
            turn.append(turn_of(turns, q))
            re, im = turned(mid, turn[-1], q, na, nr)
            cols.append(jnp.concatenate([re, im], axis=0))
        both = jnp.concatenate(cols, axis=1)
        high = both.astype(BF16)
        low = (both - high.astype(F32)).astype(BF16)
        got = dot(second, twice(high)) + dot(second[:, : 2 * nb], low)
        scale = 1.0 / (na * nb)
        for j, q in enumerate((p, p + 1)):
            spec[q, pl.ds(0, nb), :] = ((got[:nb, j * 128 : (j + 1) * 128] + delta) * scale).astype(BF16)
            spec[q, pl.ds(nb, nb), :] = (got[nb:, j * 128 : (j + 1) * 128] * scale).astype(BF16)
        if (p + 2) % step == 0:
            part = pl.ds(p + 2 - step, step)
            leave = pltpu.make_async_copy(spec.at[part], spec_out.at[part], sems.at[2 + p // step])
            leave.start()
            leaving.append(leave)
    for leave in leaving:
        leave.wait()


def conv_kernel(z, spec_in, mats_in, turns_in, out, held, data32, mid, mid_back, spec, mats, turns, sems):
    na, nr, _ = z.shape
    nb = 2 * nr
    step = na // 8
    made = copies([(mats_in, mats), (turns_in, turns)] + spec_parts(spec_in, spec, step), sems)
    spread(z, data32)
    made[0].wait()
    at = 2 * na
    first = mats[0:at, 0 : 2 * na]
    second = mats[at : at + 2 * nb, :]
    second_back = mats[at + 2 * nb : at + 4 * nb, :]
    first_back = mats[at + 4 * nb :, :]
    block_stage(data32, mid, first, na, nr)
    for p in range(0, na // 2, 2):
        if p == 0:
            made[1].wait()
        if p % step == 0:
            made[2 + p // step].wait()
        cols, turn = [], []
        for q in (p, p + 1):
            turn.append(turn_of(turns, q))
            re, im = turned(mid, turn[-1], q, na, nr)
            cols.append(jnp.concatenate([re, im], axis=0))
        got = dot(second, twice(jnp.concatenate(cols, axis=1).astype(BF16)))
        cols = []
        for j, q in enumerate((p, p + 1)):
            re, im = got[:nb, j * 128 : (j + 1) * 128], got[nb:, j * 128 : (j + 1) * 128]
            sre, sim = spec[q, pl.ds(0, nb), :].astype(F32), spec[q, pl.ds(nb, nb), :].astype(F32)
            cols.append(jnp.concatenate([re * sre - im * sim, re * sim + im * sre], axis=0))
        got = dot(second_back, twice(jnp.concatenate(cols, axis=1).astype(BF16)))
        for j, q in enumerate((p, p + 1)):
            re, im = got[:nb, j * 128 : (j + 1) * 128], got[nb:, j * 128 : (j + 1) * 128]
            tre, tim = turn[j]
            mid_back[pl.ds(q * (2 * nb + PAD), nb), :] = re * tre + im * tim
            mid_back[pl.ds(q * (2 * nb + PAD) + nb, nb), :] = im * tre - re * tim
    for r in range(0, nr, 2):
        cols = []
        for s in (r, r + 1):
            parts = []
            for ri in range(2):
                one = mid_back[pl.ds(ri * nb + s, na // 2, stride=2 * nb + PAD), :]
                two = mid_back[pl.ds(ri * nb + s + nr, na // 2, stride=2 * nb + PAD), :]
                parts.extend(lane_mix(one.astype(BF16), two.astype(BF16)))
            cols.append(jnp.concatenate(parts, axis=0))
        got = dot(first_back, twice(jnp.concatenate(cols, axis=1)))
        for j, s in enumerate((r, r + 1)):
            data32[pl.ds(s, na, stride=nr + PAD), :] = got[:, j * 128 : (j + 1) * 128]
    made = []
    for a in range(na):
        held[a] = data32[pl.ds(a * (nr + PAD), nr), :].astype(BF16)
        if (a + 1) % (na // 4) == 0:
            part = pl.ds(a + 1 - na // 4, na // 4)
            made += copies([(held.at[part], out.at[part])], sems.at[pl.ds(a // (na // 4), 1)])
    for copy in made:
        copy.wait()


def turn_filter_kernel(filt, out):
    for i in range(out.shape[0] // 2):
        block = filt[:, i * 128 : (i + 1) * 128].T
        for j in range(2):
            part = block[j * 64 : (j + 1) * 64]
            out[2 * i + j] = jnp.concatenate([part[:32], part[32:]], axis=1).astype(BF16)


def short_sum(x, halo, weights, alive):
    tok, width = x.shape
    row = lax.broadcasted_iota(jnp.int32, (tok, width), 0)
    x = jnp.where(row < alive, x.astype(F32), 0.0)
    halo = halo.astype(F32)
    before2 = jnp.where(alive > -2, halo[0:1], 0.0)
    before1 = jnp.where(alive > -1, halo[1:2], 0.0)
    back1 = jnp.where(row == 0, before1, pltpu.roll(x, 1, axis=0))
    back2 = jnp.where(row == 0, before2, jnp.where(row == 1, before1, pltpu.roll(x, 2, axis=0)))
    return weights[0:1] * x + weights[1:2] * back1 + weights[2:3] * back2


def gate_kernel(alive, rows, halo, weights, out, held, sems):
    count = rows.shape[2] // 128
    step = count // 4
    made = []
    for i in range(count):
        at = pl.ds(i * 128, 128)
        key = short_sum(rows[0, :, at], halo[1, :, at], weights[0, :, at], alive[0])
        val = short_sum(rows[1, :, at], halo[2, :, at], weights[1, :, at], alive[0])
        z = key * val
        half = z.shape[0] // 2
        one, two = lane_mix(z[:half], z[half:])
        held[2 * i] = one.astype(BF16)
        held[2 * i + 1] = two.astype(BF16)
        if (i + 1) % step == 0:
            part = pl.ds(2 * (i + 1 - step), 2 * step)
            made += copies([(held.at[part], out.at[part])], sems.at[pl.ds(i // step, 1)])
    for copy in made:
        copy.wait()


def query_kernel(alive, rows, halo, weights, out):
    for i in range(rows.shape[2] // 128):
        at = pl.ds(i * 128, 128)
        query = short_sum(rows[0, :, at], halo[0, :, at], weights[0, :, at], alive[0])
        row = lax.broadcasted_iota(jnp.int32, query.shape, 0)
        out[:, at] = jnp.where(row < alive[0], query, 0.0)


def mix_kernel(y, query, out, held, sems):
    count = out.shape[1] // 128
    step = count // 4
    made = []
    for i in range(count):
        at = pl.ds(i * 128, 128)
        top, bottom = lane_mix(y[2 * i].astype(F32), y[2 * i + 1].astype(F32))
        held[:, at] = (query[:, at] * jnp.concatenate([top, bottom], axis=0)).astype(BF16)
        if (i + 1) % step == 0:
            part = pl.ds((i + 1 - step) * 128, step * 128)
            made += copies([(held.at[:, part], out.at[:, part])], sems.at[pl.ds(i // step, 1)])
    for copy in made:
        copy.wait()


def vmem(count):
    return [pl.BlockSpec(memory_space=pltpu.VMEM)] * count


def params(limit):
    return pltpu.CompilerParams(vmem_limit_bytes=limit * 1024 * 1024)


def per_device(rows, lengths, short_weight, long_filter, filter_bias):
    tok, width = rows.shape[1], rows.shape[3]
    nseq = lax.axis_size("seq")
    ngrp = lax.axis_size("grp")
    me = lax.axis_index("seq")
    chans = width // nseq
    half = tok // 2
    span = long_filter.shape[1]
    parts = jnp.transpose(rows[0], (1, 0, 2))
    alive = lengths - me * tok
    last, long_filter = lax.optimization_barrier((parts[:, tok - 2 :, :], long_filter))
    halo = lax.ppermute(last, "seq", [(i, i + 1) for i in range(nseq - 1)])
    mats, turns = [jnp.asarray(t) for t in transform_tables(nseq, tok)]

    own = pl.pallas_call(
        turn_filter_kernel,
        out_shape=jax.ShapeDtypeStruct((span // tok, half, 2 * chans), BF16),
        in_specs=vmem(1),
        out_specs=pl.BlockSpec(memory_space=pltpu.VMEM),
        compiler_params=params(24),
        name="turn_filter",
    )(long_filter)
    group = lax.axis_index("grp")

    def from_shift(x, shift):
        return lax.ppermute(x, "grp", [((i + shift) % ngrp, i) for i in range(ngrp)])

    two = jnp.concatenate([own, from_shift(own, 4)], axis=0)
    pair = parts[1:]
    hbm = pl.BlockSpec(memory_space=pltpu.HBM)
    block = 1024
    z = pl.pallas_call(
        gate_kernel,
        out_shape=jax.ShapeDtypeStruct((nseq, half, 2 * chans), BF16),
        in_specs=[pl.BlockSpec(memory_space=pltpu.SMEM)] + vmem(3),
        out_specs=hbm,
        scratch_shapes=[
            pltpu.VMEM((nseq, half, 2 * chans), BF16),
            pltpu.SemaphoreType.DMA((4,)),
        ],
        compiler_params=params(48),
        cost_estimate=pl.CostEstimate(flops=1000000000, bytes_accessed=2000000, transcendentals=0),
        name="gate",
    )(alive, pair, halo, short_weight[1:])
    z, two = lax.optimization_barrier((z, two))
    across = [((i + (2 if i % 2 == 0 else 6)) % ngrp, i) for i in range(ngrp)]
    others = [lax.ppermute(two, "grp", across), from_shift(two, 1), from_shift(two, 7)]
    z = lax.all_to_all(z, "seq", split_axis=0, concat_axis=0, tiled=True)

    query = pl.pallas_call(
        query_kernel,
        grid=(width // block,),
        out_shape=jax.ShapeDtypeStruct((tok, width), F32),
        in_specs=[
            pl.BlockSpec(memory_space=pltpu.SMEM),
            pl.BlockSpec((1, tok, block), lambda i: (0, 0, i)),
            pl.BlockSpec((1, 2, block), lambda i: (0, 0, i)),
            pl.BlockSpec((1, 3, block), lambda i: (0, 0, i)),
        ],
        out_specs=pl.BlockSpec((tok, block), lambda i: (0, i)),
        compiler_params=params(48),
        cost_estimate=pl.CostEstimate(flops=2000000, bytes_accessed=2000000, transcendentals=0),
        name="query",
    )(alive, parts, halo, short_weight)

    table_scratch = [
        pltpu.VMEM((nseq // 2, 2 * tok, 2 * chans), BF16),
        pltpu.VMEM(mats.shape, BF16),
        pltpu.VMEM(turns.shape, F32),
    ]
    spec = pl.pallas_call(
        filter_kernel,
        out_shape=jax.ShapeDtypeStruct((nseq // 2, 2 * tok, 2 * chans), BF16),
        in_specs=[pl.BlockSpec(memory_space=pltpu.SMEM)] + vmem(5) + [hbm] * 2,
        out_specs=hbm,
        scratch_shapes=[
            pltpu.VMEM((nseq * (half + PAD), 128), F32),
            pltpu.VMEM((half * (2 * nseq + PAD), 128), F32),
            *table_scratch,
            pltpu.SemaphoreType.DMA((6,)),
        ],
        compiler_params=params(52),
        cost_estimate=pl.CostEstimate(flops=2000000000, bytes_accessed=6000000, transcendentals=0),
        name="filter_spectrum",
    )(group[None], two, *others, filter_bias[None], mats, turns)

    y = pl.pallas_call(
        conv_kernel,
        out_shape=jax.ShapeDtypeStruct((nseq, half, 2 * chans), BF16),
        in_specs=vmem(1) + [hbm] * 3,
        out_specs=hbm,
        scratch_shapes=[
            pltpu.VMEM((nseq, half, 2 * chans), BF16),
            pltpu.VMEM((nseq * (half + PAD), 128), F32),
            pltpu.VMEM((half * (2 * nseq + PAD), 128), F32),
            pltpu.VMEM((nseq // 2 * (2 * tok + PAD), 128), F32),
            *table_scratch,
            pltpu.SemaphoreType.DMA((6,)),
        ],
        compiler_params=params(52),
        name="convolve",
    )(z, spec, mats, turns)
    y = lax.all_to_all(y, "seq", split_axis=0, concat_axis=0, tiled=True)

    out = pl.pallas_call(
        mix_kernel,
        out_shape=jax.ShapeDtypeStruct((tok, width), BF16),
        in_specs=vmem(2),
        out_specs=hbm,
        scratch_shapes=[
            pltpu.VMEM((tok, width), BF16),
            pltpu.SemaphoreType.DMA((4,)),
        ],
        compiler_params=params(24),
        name="mix",
    )(y, query)
    return out[None]


def solution(mesh):
    in_specs = (P("grp", "seq", None, None), P("grp"), P(), P("seq", "grp"), P("seq"))
    out_specs = P("grp", "seq", None)
    return jax.shard_map(
        per_device, mesh=mesh, in_specs=in_specs, out_specs=out_specs, check_vma=False
    )
```

```python
import math

import jax
import jax.numpy as jnp
import numpy as np
from jax import lax
from jax.experimental import pallas as pl
from jax.experimental.pallas import tpu as pltpu
from jax.sharding import PartitionSpec as P

BF16 = jnp.bfloat16
F32 = jnp.float32
FINE = 4
PAD = 4


def split_hi_lo(table):
    high = table.astype(jnp.bfloat16)
    low = (table - high.astype(np.float64)).astype(jnp.bfloat16)
    return np.concatenate([high, low], axis=1)


def transform_tables(na, nb):
    n = na * nb
    a = np.arange(na)
    b = np.arange(nb)
    k1 = np.arange(na)
    angle = 2.0 * math.pi * np.outer(k1 + 0.25, a) / na
    first = np.concatenate([np.cos(angle), -np.sin(angle)], axis=0)
    order = np.concatenate([k1[0::2], k1[1::2]])
    back = 2.0 * math.pi * np.outer(a, order + 0.25) / na
    first_back = np.concatenate([np.cos(back), -np.sin(back)], axis=1)
    inner = 2.0 * math.pi * np.outer(b, b) / nb
    cos, sin = np.cos(inner), np.sin(inner)
    second = np.block([[cos, sin], [-sin, cos]])
    second_back = np.block([[cos, -sin], [sin, cos]])
    turn = 2.0 * math.pi * (k1[:, None] + 0.25) * b[None, :] / n
    turn = turn.reshape(na // 2, 2, nb).transpose(0, 2, 1)
    turn = np.repeat(turn, 64, axis=2)
    mats = [first, second, second_back, first_back]
    mats = [split_hi_lo(m) for m in mats]
    mats = [np.pad(m, ((0, 0), (0, 4 * nb - m.shape[1]))) for m in mats]
    factors = np.concatenate([turn[::FINE], turn[:FINE] - turn[:1]], axis=0)
    turns = np.stack([np.cos(factors), -np.sin(factors)]).astype(np.float32)
    return np.concatenate(mats, axis=0), turns


def swap_halves(x):
    return pltpu.roll(x, 64, axis=1)


def lane_mix(one, two):
    low = lax.broadcasted_iota(jnp.int32, one.shape, 1) < 64
    return (
        jnp.where(low, one, swap_halves(two)),
        jnp.where(low, swap_halves(one), two),
    )


def twice(x):
    return jnp.concatenate([x, x], axis=0)


def dot(table, x):
    return jnp.dot(table, x, preferred_element_type=F32)


def spread(data, data32):
    na, nr, _ = data.shape
    for a in range(na):
        data32[pl.ds(a * (nr + PAD), nr), :] = data[a].astype(F32)


def block_stage(data32, mid, first, na, nr):
    for r in range(0, nr, 2):
        one = data32[pl.ds(r, na, stride=nr + PAD), :]
        two = data32[pl.ds(r + 1, na, stride=nr + PAD), :]
        both = jnp.concatenate([one, two], axis=1).astype(BF16)
        got = dot(first, twice(both))
        mid[pl.ds(r * (2 * na + PAD), 2 * na), :] = got[:, :128]
        mid[pl.ds((r + 1) * (2 * na + PAD), 2 * na), :] = got[:, 128:]


def turn_of(turns, p):
    coarse = turns.shape[1] - FINE
    are, aim = turns[0, p // FINE], turns[1, p // FINE]
    if p % FINE == 0:
        return are, aim
    bre, bim = turns[0, coarse + p % FINE], turns[1, coarse + p % FINE]
    return are * bre - aim * bim, are * bim + aim * bre


def turned(mid, turn, p, na, nr):
    parts = []
    for ri in range(2):
        one = mid[pl.ds(ri * na + 2 * p, nr, stride=2 * na + PAD), :]
        two = mid[pl.ds(ri * na + 2 * p + 1, nr, stride=2 * na + PAD), :]
        top, bottom = lane_mix(one, two)
        parts.append(jnp.concatenate([top, bottom], axis=0))
    re, im = parts
    tre, tim = turn
    return re * tre - im * tim, re * tim + im * tre


def copies(pairs, sems):
    made = [pltpu.make_async_copy(src, dst, sems.at[i]) for i, (src, dst) in enumerate(pairs)]
    for copy in made:
        copy.start()
    return made


def conv_kernel(place, own, across, one_on, one_back, bias, z, mats_in, turns_in, out, held, filt32, filt_mid, data32, mid, mid_back, spec, mats, turns, sems):
    na, nr, _ = z.shape
    nb = 2 * nr
    made = copies([(mats_in, mats), (turns_in, turns)], sems)
    shards = 8
    rows = na // shards
    turned_round = 2 + 4 * lax.rem(place[0], 2)
    for source, start in ((own, 0), (across, turned_round), (one_on, 1), (one_back, 7)):
        for j in range(2):
            shard = lax.rem(place[0] + start + 4 * j, shards)
            base = pl.multiple_of(shard * (rows * (nr + PAD)), 8)
            for i in range(rows):
                filt32[pl.ds(base + i * (nr + PAD), nr), :] = source[j * rows + i].astype(F32)
    spread(z, data32)
    made[0].wait()
    at = 2 * na
    first = mats[0:at, 0 : 2 * na]
    second = mats[at : at + 2 * nb, :]
    second_back = mats[at + 2 * nb : at + 4 * nb, :]
    first_back = mats[at + 4 * nb :, :]
    block_stage(filt32, filt_mid, first, na, nr)
    block_stage(data32, mid, first, na, nr)
    made[1].wait()
    delta = bias[...]
    delta = jnp.concatenate([delta, delta], axis=1)
    scale = 1.0 / (na * nb)
    for p in range(0, na // 2, 2):
        cols = []
        for q in (p, p + 1):
            cols.append(jnp.concatenate(turned(filt_mid, turn_of(turns, q), q, na, nr), axis=0))
        got = dot(second, twice(jnp.concatenate(cols, axis=1).astype(BF16)))
        for j, q in enumerate((p, p + 1)):
            spec[q, pl.ds(0, nb), :] = (got[:nb, j * 128 : (j + 1) * 128] + delta) * scale
            spec[q, pl.ds(nb, nb), :] = got[nb:, j * 128 : (j + 1) * 128] * scale
    for p in range(0, na // 2, 2):
        cols, turn = [], []
        for q in (p, p + 1):
            turn.append(turn_of(turns, q))
            re, im = turned(mid, turn[-1], q, na, nr)
            cols.append(jnp.concatenate([re, im], axis=0))
        got = dot(second, twice(jnp.concatenate(cols, axis=1).astype(BF16)))
        cols = []
        for j, q in enumerate((p, p + 1)):
            re, im = got[:nb, j * 128 : (j + 1) * 128], got[nb:, j * 128 : (j + 1) * 128]
            sre, sim = spec[q, pl.ds(0, nb), :], spec[q, pl.ds(nb, nb), :]
            cols.append(jnp.concatenate([re * sre - im * sim, re * sim + im * sre], axis=0))
        got = dot(second_back, twice(jnp.concatenate(cols, axis=1).astype(BF16)))
        for j, q in enumerate((p, p + 1)):
            re, im = got[:nb, j * 128 : (j + 1) * 128], got[nb:, j * 128 : (j + 1) * 128]
            tre, tim = turn[j]
            mid_back[pl.ds(q * (2 * nb + PAD), nb), :] = re * tre + im * tim
            mid_back[pl.ds(q * (2 * nb + PAD) + nb, nb), :] = im * tre - re * tim
    for r in range(0, nr, 2):
        cols = []
        for s in (r, r + 1):
            parts = []
            for ri in range(2):
                one = mid_back[pl.ds(ri * nb + s, na // 2, stride=2 * nb + PAD), :]
                two = mid_back[pl.ds(ri * nb + s + nr, na // 2, stride=2 * nb + PAD), :]
                parts.extend(lane_mix(one.astype(BF16), two.astype(BF16)))
            cols.append(jnp.concatenate(parts, axis=0))
        got = dot(first_back, twice(jnp.concatenate(cols, axis=1)))
        for j, s in enumerate((r, r + 1)):
            data32[pl.ds(s, na, stride=nr + PAD), :] = got[:, j * 128 : (j + 1) * 128]
    made = []
    for a in range(na):
        held[a] = data32[pl.ds(a * (nr + PAD), nr), :].astype(BF16)
        if (a + 1) % (na // 4) == 0:
            part = pl.ds(a + 1 - na // 4, na // 4)
            made += copies([(held.at[part], out.at[part])], sems.at[pl.ds(a // (na // 4), 1)])
    for copy in made:
        copy.wait()


def turn_filter_kernel(filt, out):
    for i in range(out.shape[0] // 2):
        block = filt[:, i * 128 : (i + 1) * 128].T
        for j in range(2):
            part = block[j * 64 : (j + 1) * 64]
            out[2 * i + j] = jnp.concatenate([part[:32], part[32:]], axis=1).astype(BF16)


def short_sum(x, halo, weights, alive):
    tok, width = x.shape
    row = lax.broadcasted_iota(jnp.int32, (tok, width), 0)
    x = jnp.where(row < alive, x.astype(F32), 0.0)
    halo = halo.astype(F32)
    before2 = jnp.where(alive > -2, halo[0:1], 0.0)
    before1 = jnp.where(alive > -1, halo[1:2], 0.0)
    back1 = jnp.where(row == 0, before1, pltpu.roll(x, 1, axis=0))
    back2 = jnp.where(row == 0, before2, jnp.where(row == 1, before1, pltpu.roll(x, 2, axis=0)))
    return weights[0:1] * x + weights[1:2] * back1 + weights[2:3] * back2


def gate_kernel(alive, rows, halo, weights, out, held, sems):
    count = rows.shape[2] // 128
    step = count // 4
    made = []
    for i in range(count):
        at = pl.ds(i * 128, 128)
        key = short_sum(rows[0, :, at], halo[1, :, at], weights[0, :, at], alive[0])
        val = short_sum(rows[1, :, at], halo[2, :, at], weights[1, :, at], alive[0])
        z = key * val
        half = z.shape[0] // 2
        one, two = lane_mix(z[:half], z[half:])
        held[2 * i] = one.astype(BF16)
        held[2 * i + 1] = two.astype(BF16)
        if (i + 1) % step == 0:
            part = pl.ds(2 * (i + 1 - step), 2 * step)
            made += copies([(held.at[part], out.at[part])], sems.at[pl.ds(i // step, 1)])
    for copy in made:
        copy.wait()


def query_kernel(alive, rows, halo, weights, out):
    for i in range(rows.shape[2] // 128):
        at = pl.ds(i * 128, 128)
        query = short_sum(rows[0, :, at], halo[0, :, at], weights[0, :, at], alive[0])
        row = lax.broadcasted_iota(jnp.int32, query.shape, 0)
        out[:, at] = jnp.where(row < alive[0], query, 0.0)


def mix_kernel(y, query, out, held, sems):
    count = out.shape[1] // 128
    step = count // 4
    made = []
    for i in range(count):
        at = pl.ds(i * 128, 128)
        top, bottom = lane_mix(y[2 * i].astype(F32), y[2 * i + 1].astype(F32))
        held[:, at] = (query[:, at] * jnp.concatenate([top, bottom], axis=0)).astype(BF16)
        if (i + 1) % step == 0:
            part = pl.ds((i + 1 - step) * 128, step * 128)
            made += copies([(held.at[:, part], out.at[:, part])], sems.at[pl.ds(i // step, 1)])
    for copy in made:
        copy.wait()


def vmem(count):
    return [pl.BlockSpec(memory_space=pltpu.VMEM)] * count


def params(limit):
    return pltpu.CompilerParams(vmem_limit_bytes=limit * 1024 * 1024)


def per_device(rows, lengths, short_weight, long_filter, filter_bias):
    tok, width = rows.shape[1], rows.shape[3]
    nseq = lax.axis_size("seq")
    ngrp = lax.axis_size("grp")
    me = lax.axis_index("seq")
    chans = width // nseq
    half = tok // 2
    span = long_filter.shape[1]
    parts = jnp.transpose(rows[0], (1, 0, 2))
    alive = lengths - me * tok
    last, long_filter = lax.optimization_barrier((parts[:, tok - 2 :, :], long_filter))
    halo = lax.ppermute(last, "seq", [(i, i + 1) for i in range(nseq - 1)])
    mats, turns = [jnp.asarray(t) for t in transform_tables(nseq, tok)]

    own = pl.pallas_call(
        turn_filter_kernel,
        out_shape=jax.ShapeDtypeStruct((span // tok, half, 2 * chans), BF16),
        in_specs=vmem(1),
        out_specs=pl.BlockSpec(memory_space=pltpu.VMEM),
        compiler_params=params(24),
        name="turn_filter",
    )(long_filter)
    group = lax.axis_index("grp")

    def from_shift(x, shift):
        return lax.ppermute(x, "grp", [((i + shift) % ngrp, i) for i in range(ngrp)])

    two = jnp.concatenate([own, from_shift(own, 4)], axis=0)
    pair = parts[1:]
    hbm = pl.BlockSpec(memory_space=pltpu.HBM)
    block = 1024
    z = pl.pallas_call(
        gate_kernel,
        out_shape=jax.ShapeDtypeStruct((nseq, half, 2 * chans), BF16),
        in_specs=[pl.BlockSpec(memory_space=pltpu.SMEM)] + vmem(3),
        out_specs=hbm,
        scratch_shapes=[
            pltpu.VMEM((nseq, half, 2 * chans), BF16),
            pltpu.SemaphoreType.DMA((4,)),
        ],
        compiler_params=params(48),
        cost_estimate=pl.CostEstimate(flops=1000000000, bytes_accessed=2000000, transcendentals=0),
        name="gate",
    )(alive, pair, halo, short_weight[1:])
    z, two = lax.optimization_barrier((z, two))
    across = [((i + (2 if i % 2 == 0 else 6)) % ngrp, i) for i in range(ngrp)]
    others = [lax.ppermute(two, "grp", across), from_shift(two, 1), from_shift(two, 7)]
    z = lax.all_to_all(z, "seq", split_axis=0, concat_axis=0, tiled=True)

    query = pl.pallas_call(
        query_kernel,
        grid=(width // block,),
        out_shape=jax.ShapeDtypeStruct((tok, width), F32),
        in_specs=[
            pl.BlockSpec(memory_space=pltpu.SMEM),
            pl.BlockSpec((1, tok, block), lambda i: (0, 0, i)),
            pl.BlockSpec((1, 2, block), lambda i: (0, 0, i)),
            pl.BlockSpec((1, 3, block), lambda i: (0, 0, i)),
        ],
        out_specs=pl.BlockSpec((tok, block), lambda i: (0, i)),
        compiler_params=params(48),
        cost_estimate=pl.CostEstimate(flops=2000000, bytes_accessed=2000000, transcendentals=0),
        name="query",
    )(alive, parts, halo, short_weight)

    table_scratch = [
        pltpu.VMEM((nseq // 2, 2 * tok, 2 * chans), F32),
        pltpu.VMEM(mats.shape, BF16),
        pltpu.VMEM(turns.shape, F32),
    ]
    y = pl.pallas_call(
        conv_kernel,
        out_shape=jax.ShapeDtypeStruct((nseq, half, 2 * chans), BF16),
        in_specs=[pl.BlockSpec(memory_space=pltpu.SMEM)] + vmem(6) + [hbm] * 2,
        out_specs=hbm,
        scratch_shapes=[
            pltpu.VMEM((nseq, half, 2 * chans), BF16),
            pltpu.VMEM((nseq * (half + PAD), 128), F32),
            pltpu.VMEM((half * (2 * nseq + PAD), 128), F32),
            pltpu.VMEM((nseq * (half + PAD), 128), F32),
            pltpu.VMEM((half * (2 * nseq + PAD), 128), F32),
            pltpu.VMEM((nseq // 2 * (2 * tok + PAD), 128), F32),
            *table_scratch,
            pltpu.SemaphoreType.DMA((4,)),
        ],
        compiler_params=params(52),
        name="convolve",
    )(group[None], two, *others, filter_bias[None], z, mats, turns)
    y = lax.all_to_all(y, "seq", split_axis=0, concat_axis=0, tiled=True)

    out = pl.pallas_call(
        mix_kernel,
        out_shape=jax.ShapeDtypeStruct((tok, width), BF16),
        in_specs=vmem(2),
        out_specs=hbm,
        scratch_shapes=[
            pltpu.VMEM((tok, width), BF16),
            pltpu.SemaphoreType.DMA((4,)),
        ],
        compiler_params=params(24),
        name="mix",
    )(y, query)
    return out[None]


def solution(mesh):
    in_specs = (P("grp", "seq", None, None), P("grp"), P(), P("seq", "grp"), P("seq"))
    out_specs = P("grp", "seq", None)
    return jax.shard_map(
        per_device, mesh=mesh, in_specs=in_specs, out_specs=out_specs, check_vma=False
    )
```

```python
import math

import jax
import jax.numpy as jnp
import numpy as np
from jax import lax
from jax.experimental import pallas as pl
from jax.experimental.pallas import tpu as pltpu
from jax.sharding import PartitionSpec as P

BF16 = jnp.bfloat16
F32 = jnp.float32
FINE = 4
PAD = 4


def split_hi_lo(table):
    high = table.astype(jnp.bfloat16)
    low = (table - high.astype(np.float64)).astype(jnp.bfloat16)
    return np.concatenate([high, low], axis=1)


def transform_tables(na, nb):
    n = na * nb
    a = np.arange(na)
    b = np.arange(nb)
    k1 = np.arange(na)
    angle = 2.0 * math.pi * np.outer(k1 + 0.25, a) / na
    first = np.concatenate([np.cos(angle), -np.sin(angle)], axis=0)
    order = np.concatenate([k1[0::2], k1[1::2]])
    back = 2.0 * math.pi * np.outer(a, order + 0.25) / na
    first_back = np.concatenate([np.cos(back), -np.sin(back)], axis=1)
    inner = 2.0 * math.pi * np.outer(b, b) / nb
    cos, sin = np.cos(inner), np.sin(inner)
    second = np.block([[cos, sin], [-sin, cos]])
    second_back = np.block([[cos, -sin], [sin, cos]])
    turn = 2.0 * math.pi * (k1[:, None] + 0.25) * b[None, :] / n
    turn = turn.reshape(na // 2, 2, nb).transpose(0, 2, 1)
    turn = np.repeat(turn, 64, axis=2)
    mats = [first, second, second_back, first_back]
    mats = [split_hi_lo(m) for m in mats]
    mats = [np.pad(m, ((0, 0), (0, 4 * nb - m.shape[1]))) for m in mats]
    factors = np.concatenate([turn[::FINE], turn[:FINE] - turn[:1]], axis=0)
    turns = np.stack([np.cos(factors), -np.sin(factors)]).astype(np.float32)
    return np.concatenate(mats, axis=0), turns


def swap_halves(x):
    return pltpu.roll(x, 64, axis=1)


def lane_mix(one, two):
    low = lax.broadcasted_iota(jnp.int32, one.shape, 1) < 64
    return (
        jnp.where(low, one, swap_halves(two)),
        jnp.where(low, swap_halves(one), two),
    )


def twice(x):
    return jnp.concatenate([x, x], axis=0)


def dot(table, x):
    return jnp.dot(table, x, preferred_element_type=F32)


def spread(data, data32):
    na, nr, _ = data.shape
    for a in range(na):
        data32[pl.ds(a * (nr + PAD), nr), :] = data[a].astype(F32)


def block_stage(data32, mid, first, na, nr):
    for r in range(0, nr, 2):
        one = data32[pl.ds(r, na, stride=nr + PAD), :]
        two = data32[pl.ds(r + 1, na, stride=nr + PAD), :]
        both = jnp.concatenate([one, two], axis=1).astype(BF16)
        got = dot(first, twice(both))
        mid[pl.ds(r * (2 * na + PAD), 2 * na), :] = got[:, :128]
        mid[pl.ds((r + 1) * (2 * na + PAD), 2 * na), :] = got[:, 128:]


def turn_of(turns, p):
    coarse = turns.shape[1] - FINE
    are, aim = turns[0, p // FINE], turns[1, p // FINE]
    if p % FINE == 0:
        return are, aim
    bre, bim = turns[0, coarse + p % FINE], turns[1, coarse + p % FINE]
    return are * bre - aim * bim, are * bim + aim * bre


def turned(mid, turn, p, na, nr):
    parts = []
    for ri in range(2):
        one = mid[pl.ds(ri * na + 2 * p, nr, stride=2 * na + PAD), :]
        two = mid[pl.ds(ri * na + 2 * p + 1, nr, stride=2 * na + PAD), :]
        top, bottom = lane_mix(one, two)
        parts.append(jnp.concatenate([top, bottom], axis=0))
    re, im = parts
    tre, tim = turn
    return re * tre - im * tim, re * tim + im * tre


def copies(pairs, sems):
    made = [pltpu.make_async_copy(src, dst, sems.at[i]) for i, (src, dst) in enumerate(pairs)]
    for copy in made:
        copy.start()
    return made


def conv_kernel(place, own, across, one_on, one_back, bias, z, mats_in, turns_in, out, held, filt32, filt_mid, data32, mid, mid_back, spec, mats, turns, sems):
    na, nr, _ = z.shape
    nb = 2 * nr
    made = copies([(mats_in, mats), (turns_in, turns)], sems)
    shards = 8
    rows = na // shards
    turned_round = 2 + 4 * lax.rem(place[0], 2)
    for source, start in ((own, 0), (across, turned_round), (one_on, 1), (one_back, 7)):
        for j in range(2):
            shard = lax.rem(place[0] + start + 4 * j, shards)
            base = pl.multiple_of(shard * (rows * (nr + PAD)), 8)
            for i in range(rows):
                filt32[pl.ds(base + i * (nr + PAD), nr), :] = source[j * rows + i].astype(F32)
    spread(z, data32)
    made[0].wait()
    at = 2 * na
    first = mats[0:at, 0 : 2 * na]
    second = mats[at : at + 2 * nb, :]
    second_back = mats[at + 2 * nb : at + 4 * nb, :]
    first_back = mats[at + 4 * nb :, :]
    block_stage(filt32, filt_mid, first, na, nr)
    block_stage(data32, mid, first, na, nr)
    made[1].wait()
    delta = bias[...]
    delta = jnp.concatenate([delta, delta], axis=1)
    scale = 1.0 / (na * nb)
    for p in range(0, na // 2, 2):
        cols = []
        for q in (p, p + 1):
            cols.append(jnp.concatenate(turned(filt_mid, turn_of(turns, q), q, na, nr), axis=0))
        got = dot(second, twice(jnp.concatenate(cols, axis=1).astype(BF16)))
        for j, q in enumerate((p, p + 1)):
            spec[q, pl.ds(0, nb), :] = (got[:nb, j * 128 : (j + 1) * 128] + delta) * scale
            spec[q, pl.ds(nb, nb), :] = got[nb:, j * 128 : (j + 1) * 128] * scale
    for p in range(0, na // 2, 2):
        cols, turn = [], []
        for q in (p, p + 1):
            turn.append(turn_of(turns, q))
            re, im = turned(mid, turn[-1], q, na, nr)
            cols.append(jnp.concatenate([re, im], axis=0))
        got = dot(second, twice(jnp.concatenate(cols, axis=1).astype(BF16)))
        cols = []
        for j, q in enumerate((p, p + 1)):
            re, im = got[:nb, j * 128 : (j + 1) * 128], got[nb:, j * 128 : (j + 1) * 128]
            sre, sim = spec[q, pl.ds(0, nb), :], spec[q, pl.ds(nb, nb), :]
            cols.append(jnp.concatenate([re * sre - im * sim, re * sim + im * sre], axis=0))
        got = dot(second_back, twice(jnp.concatenate(cols, axis=1).astype(BF16)))
        for j, q in enumerate((p, p + 1)):
            re, im = got[:nb, j * 128 : (j + 1) * 128], got[nb:, j * 128 : (j + 1) * 128]
            tre, tim = turn[j]
            mid_back[pl.ds(q * (2 * nb + PAD), nb), :] = re * tre + im * tim
            mid_back[pl.ds(q * (2 * nb + PAD) + nb, nb), :] = im * tre - re * tim
    for r in range(0, nr, 2):
        cols = []
        for s in (r, r + 1):
            parts = []
            for ri in range(2):
                one = mid_back[pl.ds(ri * nb + s, na // 2, stride=2 * nb + PAD), :]
                two = mid_back[pl.ds(ri * nb + s + nr, na // 2, stride=2 * nb + PAD), :]
                parts.extend(lane_mix(one.astype(BF16), two.astype(BF16)))
            cols.append(jnp.concatenate(parts, axis=0))
        got = dot(first_back, twice(jnp.concatenate(cols, axis=1)))
        for j, s in enumerate((r, r + 1)):
            data32[pl.ds(s, na, stride=nr + PAD), :] = got[:, j * 128 : (j + 1) * 128]
    made = []
    for a in range(na):
        held[a] = data32[pl.ds(a * (nr + PAD), nr), :].astype(BF16)
        if (a + 1) % (na // 4) == 0:
            part = pl.ds(a + 1 - na // 4, na // 4)
            made += copies([(held.at[part], out.at[part])], sems.at[pl.ds(a // (na // 4), 1)])
    for copy in made:
        copy.wait()


def turn_filter_kernel(filt, out):
    for i in range(out.shape[0] // 2):
        block = filt[:, i * 128 : (i + 1) * 128].T
        for j in range(2):
            part = block[j * 64 : (j + 1) * 64]
            out[2 * i + j] = jnp.concatenate([part[:32], part[32:]], axis=1).astype(BF16)


def short_sum(x, halo, weights, alive):
    tok, width = x.shape
    row = lax.broadcasted_iota(jnp.int32, (tok, width), 0)
    x = jnp.where(row < alive, x.astype(F32), 0.0)
    halo = halo.astype(F32)
    before2 = jnp.where(alive > -2, halo[0:1], 0.0)
    before1 = jnp.where(alive > -1, halo[1:2], 0.0)
    back1 = jnp.where(row == 0, before1, pltpu.roll(x, 1, axis=0))
    back2 = jnp.where(row == 0, before2, jnp.where(row == 1, before1, pltpu.roll(x, 2, axis=0)))
    return weights[0:1] * x + weights[1:2] * back1 + weights[2:3] * back2


def gate_kernel(alive, rows_in, halo, weights_in, out, rows, weights, held, in_sems, sems):
    count = rows.shape[2] // 128
    step = count // 4
    spans = [pl.ds(i * step * 128, step * 128) for i in range(4)]
    coming = copies([(weights_in, weights)] + [(rows_in.at[pl.ds(1, 2), :, span], rows.at[:, :, span]) for span in spans], in_sems)
    coming[0].wait()
    made = []
    for i in range(count):
        if i % step == 0:
            coming[1 + i // step].wait()
        at = pl.ds(i * 128, 128)
        key = short_sum(rows[0, :, at], halo[1, :, at], weights[1, :, at], alive[0])
        val = short_sum(rows[1, :, at], halo[2, :, at], weights[2, :, at], alive[0])
        z = key * val
        half = z.shape[0] // 2
        one, two = lane_mix(z[:half], z[half:])
        held[2 * i] = one.astype(BF16)
        held[2 * i + 1] = two.astype(BF16)
        if (i + 1) % step == 0:
            part = pl.ds(2 * (i + 1 - step), 2 * step)
            made += copies([(held.at[part], out.at[part])], sems.at[pl.ds(i // step, 1)])
    for copy in made:
        copy.wait()


def query_kernel(alive, rows, halo, weights, out):
    for i in range(rows.shape[2] // 128):
        at = pl.ds(i * 128, 128)
        query = short_sum(rows[0, :, at], halo[0, :, at], weights[0, :, at], alive[0])
        row = lax.broadcasted_iota(jnp.int32, query.shape, 0)
        out[:, at] = jnp.where(row < alive[0], query, 0.0)


def mix_kernel(y, query, out, held, sems):
    count = out.shape[1] // 128
    step = count // 4
    made = []
    for i in range(count):
        at = pl.ds(i * 128, 128)
        top, bottom = lane_mix(y[2 * i].astype(F32), y[2 * i + 1].astype(F32))
        held[:, at] = (query[:, at] * jnp.concatenate([top, bottom], axis=0)).astype(BF16)
        if (i + 1) % step == 0:
            part = pl.ds((i + 1 - step) * 128, step * 128)
            made += copies([(held.at[:, part], out.at[:, part])], sems.at[pl.ds(i // step, 1)])
    for copy in made:
        copy.wait()


def vmem(count):
    return [pl.BlockSpec(memory_space=pltpu.VMEM)] * count


def params(limit):
    return pltpu.CompilerParams(vmem_limit_bytes=limit * 1024 * 1024)


def per_device(rows, lengths, short_weight, long_filter, filter_bias):
    tok, width = rows.shape[1], rows.shape[3]
    nseq = lax.axis_size("seq")
    ngrp = lax.axis_size("grp")
    me = lax.axis_index("seq")
    chans = width // nseq
    half = tok // 2
    span = long_filter.shape[1]
    parts = jnp.transpose(rows[0], (1, 0, 2))
    alive = lengths - me * tok
    halo = lax.ppermute(parts[:, tok - 2 :, :], "seq", [(i, i + 1) for i in range(nseq - 1)])
    mats, turns = [jnp.asarray(t) for t in transform_tables(nseq, tok)]

    own = pl.pallas_call(
        turn_filter_kernel,
        out_shape=jax.ShapeDtypeStruct((span // tok, half, 2 * chans), BF16),
        in_specs=vmem(1),
        out_specs=pl.BlockSpec(memory_space=pltpu.VMEM),
        compiler_params=params(24),
        name="turn_filter",
    )(long_filter)
    group = lax.axis_index("grp")

    def from_shift(x, shift):
        return lax.ppermute(x, "grp", [((i + shift) % ngrp, i) for i in range(ngrp)])

    two = jnp.concatenate([own, from_shift(own, 4)], axis=0)
    hbm = pl.BlockSpec(memory_space=pltpu.HBM)
    block = 1024
    z = pl.pallas_call(
        gate_kernel,
        out_shape=jax.ShapeDtypeStruct((nseq, half, 2 * chans), BF16),
        in_specs=[pl.BlockSpec(memory_space=pltpu.SMEM), hbm] + vmem(1) + [hbm],
        out_specs=hbm,
        scratch_shapes=[
            pltpu.VMEM((2, tok, width), BF16),
            pltpu.VMEM(short_weight.shape, F32),
            pltpu.VMEM((nseq, half, 2 * chans), BF16),
            pltpu.SemaphoreType.DMA((5,)),
            pltpu.SemaphoreType.DMA((4,)),
        ],
        compiler_params=params(53),
        cost_estimate=pl.CostEstimate(flops=1000000000, bytes_accessed=2000000, transcendentals=0),
        name="gate",
    )(alive, parts, halo, short_weight)
    z, two = lax.optimization_barrier((z, two))
    across = [((i + (2 if i % 2 == 0 else 6)) % ngrp, i) for i in range(ngrp)]
    others = [lax.ppermute(two, "grp", across), from_shift(two, 1), from_shift(two, 7)]
    z = lax.all_to_all(z, "seq", split_axis=0, concat_axis=0, tiled=True)

    query = pl.pallas_call(
        query_kernel,
        grid=(width // block,),
        out_shape=jax.ShapeDtypeStruct((tok, width), F32),
        in_specs=[
            pl.BlockSpec(memory_space=pltpu.SMEM),
            pl.BlockSpec((1, tok, block), lambda i: (0, 0, i)),
            pl.BlockSpec((1, 2, block), lambda i: (0, 0, i)),
            pl.BlockSpec((1, 3, block), lambda i: (0, 0, i)),
        ],
        out_specs=pl.BlockSpec((tok, block), lambda i: (0, i)),
        compiler_params=params(48),
        cost_estimate=pl.CostEstimate(flops=2000000, bytes_accessed=2000000, transcendentals=0),
        name="query",
    )(alive, parts, halo, short_weight)

    table_scratch = [
        pltpu.VMEM((nseq // 2, 2 * tok, 2 * chans), F32),
        pltpu.VMEM(mats.shape, BF16),
        pltpu.VMEM(turns.shape, F32),
    ]
    y = pl.pallas_call(
        conv_kernel,
        out_shape=jax.ShapeDtypeStruct((nseq, half, 2 * chans), BF16),
        in_specs=[pl.BlockSpec(memory_space=pltpu.SMEM)] + vmem(6) + [hbm] * 2,
        out_specs=hbm,
        scratch_shapes=[
            pltpu.VMEM((nseq, half, 2 * chans), BF16),
            pltpu.VMEM((nseq * (half + PAD), 128), F32),
            pltpu.VMEM((half * (2 * nseq + PAD), 128), F32),
            pltpu.VMEM((nseq * (half + PAD), 128), F32),
            pltpu.VMEM((half * (2 * nseq + PAD), 128), F32),
            pltpu.VMEM((nseq // 2 * (2 * tok + PAD), 128), F32),
            *table_scratch,
            pltpu.SemaphoreType.DMA((4,)),
        ],
        compiler_params=params(52),
        name="convolve",
    )(group[None], two, *others, filter_bias[None], z, mats, turns)
    y = lax.all_to_all(y, "seq", split_axis=0, concat_axis=0, tiled=True)

    out = pl.pallas_call(
        mix_kernel,
        out_shape=jax.ShapeDtypeStruct((tok, width), BF16),
        in_specs=vmem(2),
        out_specs=hbm,
        scratch_shapes=[
            pltpu.VMEM((tok, width), BF16),
            pltpu.SemaphoreType.DMA((4,)),
        ],
        compiler_params=params(24),
        name="mix",
    )(y, query)
    return out[None]


def solution(mesh):
    in_specs = (P("grp", "seq", None, None), P("grp"), P(), P("seq", "grp"), P("seq"))
    out_specs = P("grp", "seq", None)
    return jax.shard_map(
        per_device, mesh=mesh, in_specs=in_specs, out_specs=out_specs, check_vma=False
    )
```

```python
import math

import jax
import jax.numpy as jnp
import numpy as np
from jax import lax
from jax.experimental import pallas as pl
from jax.experimental.pallas import tpu as pltpu
from jax.sharding import PartitionSpec as P

BF16 = jnp.bfloat16
F32 = jnp.float32
FINE = 4
PAD = 4


def split_hi_lo(table):
    high = table.astype(jnp.bfloat16)
    low = (table - high.astype(np.float64)).astype(jnp.bfloat16)
    return np.concatenate([high, low], axis=1)


def transform_tables(na, nb):
    n = na * nb
    a = np.arange(na)
    b = np.arange(nb)
    k1 = np.arange(na)
    angle = 2.0 * math.pi * np.outer(k1 + 0.25, a) / na
    first = np.concatenate([np.cos(angle), -np.sin(angle)], axis=0)
    order = np.concatenate([k1[0::2], k1[1::2]])
    back = 2.0 * math.pi * np.outer(a, order + 0.25) / na
    first_back = np.concatenate([np.cos(back), -np.sin(back)], axis=1)
    inner = 2.0 * math.pi * np.outer(b, b) / nb
    cos, sin = np.cos(inner), np.sin(inner)
    second = np.block([[cos, sin], [-sin, cos]])
    second_back = np.block([[cos, -sin], [sin, cos]])
    turn = 2.0 * math.pi * (k1[:, None] + 0.25) * b[None, :] / n
    turn = turn.reshape(na // 2, 2, nb).transpose(0, 2, 1)
    turn = np.repeat(turn, 64, axis=2)
    mats = [first, second, second_back, first_back]
    mats = [split_hi_lo(m) for m in mats]
    mats = [np.pad(m, ((0, 0), (0, 4 * nb - m.shape[1]))) for m in mats]
    factors = np.concatenate([turn[::FINE], turn[:FINE] - turn[:1]], axis=0)
    turns = np.stack([np.cos(factors), -np.sin(factors)]).astype(np.float32)
    return np.concatenate(mats, axis=0), turns


def swap_halves(x):
    return pltpu.roll(x, 64, axis=1)


def lane_mix(one, two):
    low = lax.broadcasted_iota(jnp.int32, one.shape, 1) < 64
    return (
        jnp.where(low, one, swap_halves(two)),
        jnp.where(low, swap_halves(one), two),
    )


def twice(x):
    return jnp.concatenate([x, x], axis=0)


def dot(table, x):
    return jnp.dot(table, x, preferred_element_type=F32)


def spread(data, data32):
    na, nr, _ = data.shape
    for a in range(na):
        data32[pl.ds(a * (nr + PAD), nr), :] = data[a].astype(F32)


def block_stage(data32, mid, first, na, nr):
    for r in range(0, nr, 2):
        one = data32[pl.ds(r, na, stride=nr + PAD), :]
        two = data32[pl.ds(r + 1, na, stride=nr + PAD), :]
        both = jnp.concatenate([one, two], axis=1).astype(BF16)
        got = dot(first, twice(both))
        mid[pl.ds(r * (2 * na + PAD), 2 * na), :] = got[:, :128]
        mid[pl.ds((r + 1) * (2 * na + PAD), 2 * na), :] = got[:, 128:]


def turn_of(turns, p):
    coarse = turns.shape[1] - FINE
    are, aim = turns[0, p // FINE], turns[1, p // FINE]
    if p % FINE == 0:
        return are, aim
    bre, bim = turns[0, coarse + p % FINE], turns[1, coarse + p % FINE]
    return are * bre - aim * bim, are * bim + aim * bre


def turned(mid, turn, p, na, nr):
    parts = []
    for ri in range(2):
        one = mid[pl.ds(ri * na + 2 * p, nr, stride=2 * na + PAD), :]
        two = mid[pl.ds(ri * na + 2 * p + 1, nr, stride=2 * na + PAD), :]
        top, bottom = lane_mix(one, two)
        parts.append(jnp.concatenate([top, bottom], axis=0))
    re, im = parts
    tre, tim = turn
    return re * tre - im * tim, re * tim + im * tre


def copies(pairs, sems):
    made = [pltpu.make_async_copy(src, dst, sems.at[i]) for i, (src, dst) in enumerate(pairs)]
    for copy in made:
        copy.start()
    return made


def conv_kernel(place, own, across, one_on, one_back, bias, z, mats_in, turns_in, out, held, filt32, filt_mid, data32, mid, mid_back, spec, mats, turns, sems):
    na, nr, _ = z.shape
    nb = 2 * nr
    made = copies([(mats_in, mats), (turns_in, turns)], sems)
    shards = 8
    rows = na // shards
    turned_round = 2 + 4 * lax.rem(place[0], 2)
    for source, start in ((own, 0), (across, turned_round), (one_on, 1), (one_back, 7)):
        for j in range(2):
            shard = lax.rem(place[0] + start + 4 * j, shards)
            base = pl.multiple_of(shard * (rows * (nr + PAD)), 8)
            for i in range(rows):
                filt32[pl.ds(base + i * (nr + PAD), nr), :] = source[j * rows + i].astype(F32)
    spread(z, data32)
    made[0].wait()
    at = 2 * na
    first = mats[0:at, 0 : 2 * na]
    second = mats[at : at + 2 * nb, :]
    second_back = mats[at + 2 * nb : at + 4 * nb, :]
    first_back = mats[at + 4 * nb :, :]
    block_stage(filt32, filt_mid, first, na, nr)
    block_stage(data32, mid, first, na, nr)
    made[1].wait()
    delta = bias[...]
    delta = jnp.concatenate([delta, delta], axis=1)
    scale = 1.0 / (na * nb)
    for p in range(0, na // 2, 2):
        cols = []
        for q in (p, p + 1):
            cols.append(jnp.concatenate(turned(filt_mid, turn_of(turns, q), q, na, nr), axis=0))
        got = dot(second, twice(jnp.concatenate(cols, axis=1).astype(BF16)))
        for j, q in enumerate((p, p + 1)):
            spec[q, pl.ds(0, nb), :] = (got[:nb, j * 128 : (j + 1) * 128] + delta) * scale
            spec[q, pl.ds(nb, nb), :] = got[nb:, j * 128 : (j + 1) * 128] * scale
    for p in range(0, na // 2, 2):
        cols, turn = [], []
        for q in (p, p + 1):
            turn.append(turn_of(turns, q))
            re, im = turned(mid, turn[-1], q, na, nr)
            cols.append(jnp.concatenate([re, im], axis=0))
        got = dot(second, twice(jnp.concatenate(cols, axis=1).astype(BF16)))
        cols = []
        for j, q in enumerate((p, p + 1)):
            re, im = got[:nb, j * 128 : (j + 1) * 128], got[nb:, j * 128 : (j + 1) * 128]
            sre, sim = spec[q, pl.ds(0, nb), :], spec[q, pl.ds(nb, nb), :]
            cols.append(jnp.concatenate([re * sre - im * sim, re * sim + im * sre], axis=0))
        got = dot(second_back, twice(jnp.concatenate(cols, axis=1).astype(BF16)))
        for j, q in enumerate((p, p + 1)):
            re, im = got[:nb, j * 128 : (j + 1) * 128], got[nb:, j * 128 : (j + 1) * 128]
            tre, tim = turn[j]
            mid_back[pl.ds(q * (2 * nb + PAD), nb), :] = re * tre + im * tim
            mid_back[pl.ds(q * (2 * nb + PAD) + nb, nb), :] = im * tre - re * tim
    for r in range(0, nr, 2):
        cols = []
        for s in (r, r + 1):
            parts = []
            for ri in range(2):
                one = mid_back[pl.ds(ri * nb + s, na // 2, stride=2 * nb + PAD), :]
                two = mid_back[pl.ds(ri * nb + s + nr, na // 2, stride=2 * nb + PAD), :]
                parts.extend(lane_mix(one.astype(BF16), two.astype(BF16)))
            cols.append(jnp.concatenate(parts, axis=0))
        got = dot(first_back, twice(jnp.concatenate(cols, axis=1)))
        for j, s in enumerate((r, r + 1)):
            data32[pl.ds(s, na, stride=nr + PAD), :] = got[:, j * 128 : (j + 1) * 128]
    made = []
    for a in range(na):
        held[a] = data32[pl.ds(a * (nr + PAD), nr), :].astype(BF16)
        if (a + 1) % (na // 4) == 0:
            part = pl.ds(a + 1 - na // 4, na // 4)
            made += copies([(held.at[part], out.at[part])], sems.at[pl.ds(a // (na // 4), 1)])
    for copy in made:
        copy.wait()


def head_kernel(parts, filt_in, own, last, tail, filt, sems):
    rows = tail.shape[1]
    made = copies([(parts.at[:, pl.ds(parts.shape[1] - rows, rows), :], tail), (filt_in, filt)], sems)
    made[0].wait()
    last[...] = tail[:, rows - 2 :, :]
    made[1].wait()
    for i in range(own.shape[0] // 2):
        block = filt[:, i * 128 : (i + 1) * 128].T
        for j in range(2):
            part = block[j * 64 : (j + 1) * 64]
            own[2 * i + j] = jnp.concatenate([part[:32], part[32:]], axis=1).astype(BF16)


def short_sum(x, halo, weights, alive):
    tok, width = x.shape
    row = lax.broadcasted_iota(jnp.int32, (tok, width), 0)
    x = jnp.where(row < alive, x.astype(F32), 0.0)
    halo = halo.astype(F32)
    before2 = jnp.where(alive > -2, halo[0:1], 0.0)
    before1 = jnp.where(alive > -1, halo[1:2], 0.0)
    back1 = jnp.where(row == 0, before1, pltpu.roll(x, 1, axis=0))
    back2 = jnp.where(row == 0, before2, jnp.where(row == 1, before1, pltpu.roll(x, 2, axis=0)))
    return weights[0:1] * x + weights[1:2] * back1 + weights[2:3] * back2


def gate_kernel(alive, rows_in, halo, weights_in, out, rows, weights, held, in_sems, sems):
    count = rows.shape[2] // 128
    step = count // 4
    spans = [pl.ds(i * step * 128, step * 128) for i in range(4)]
    coming = copies([(weights_in, weights)] + [(rows_in.at[pl.ds(1, 2), :, span], rows.at[:, :, span]) for span in spans], in_sems)
    coming[0].wait()
    made = []
    for i in range(count):
        if i % step == 0:
            coming[1 + i // step].wait()
        at = pl.ds(i * 128, 128)
        key = short_sum(rows[0, :, at], halo[1, :, at], weights[1, :, at], alive[0])
        val = short_sum(rows[1, :, at], halo[2, :, at], weights[2, :, at], alive[0])
        z = key * val
        half = z.shape[0] // 2
        one, two = lane_mix(z[:half], z[half:])
        held[2 * i] = one.astype(BF16)
        held[2 * i + 1] = two.astype(BF16)
        if (i + 1) % step == 0:
            part = pl.ds(2 * (i + 1 - step), 2 * step)
            made += copies([(held.at[part], out.at[part])], sems.at[pl.ds(i // step, 1)])
    for copy in made:
        copy.wait()


def query_kernel(alive, rows, halo, weights, out):
    for i in range(rows.shape[2] // 128):
        at = pl.ds(i * 128, 128)
        query = short_sum(rows[0, :, at], halo[0, :, at], weights[0, :, at], alive[0])
        row = lax.broadcasted_iota(jnp.int32, query.shape, 0)
        out[:, at] = jnp.where(row < alive[0], query, 0.0)


def mix_kernel(y, query, out, held, sems):
    count = out.shape[1] // 128
    step = count // 4
    made = []
    for i in range(count):
        at = pl.ds(i * 128, 128)
        top, bottom = lane_mix(y[2 * i].astype(F32), y[2 * i + 1].astype(F32))
        held[:, at] = (query[:, at] * jnp.concatenate([top, bottom], axis=0)).astype(BF16)
        if (i + 1) % step == 0:
            part = pl.ds((i + 1 - step) * 128, step * 128)
            made += copies([(held.at[:, part], out.at[:, part])], sems.at[pl.ds(i // step, 1)])
    for copy in made:
        copy.wait()


def vmem(count):
    return [pl.BlockSpec(memory_space=pltpu.VMEM)] * count


def params(limit):
    return pltpu.CompilerParams(vmem_limit_bytes=int(limit * 1024 * 1024))


def per_device(rows, lengths, short_weight, long_filter, filter_bias):
    tok, width = rows.shape[1], rows.shape[3]
    nseq = lax.axis_size("seq")
    ngrp = lax.axis_size("grp")
    me = lax.axis_index("seq")
    chans = width // nseq
    half = tok // 2
    span = long_filter.shape[1]
    parts = jnp.transpose(rows[0], (1, 0, 2))
    alive = lengths - me * tok
    mats, turns = [jnp.asarray(t) for t in transform_tables(nseq, tok)]

    hbm = pl.BlockSpec(memory_space=pltpu.HBM)
    own, last = pl.pallas_call(
        head_kernel,
        out_shape=(
            jax.ShapeDtypeStruct((span // tok, half, 2 * chans), BF16),
            jax.ShapeDtypeStruct((3, 2, width), BF16),
        ),
        in_specs=[hbm] * 2,
        out_specs=tuple(vmem(2)),
        scratch_shapes=[
            pltpu.VMEM((3, 16, width), BF16),
            pltpu.VMEM(long_filter.shape, F32),
            pltpu.SemaphoreType.DMA((2,)),
        ],
        compiler_params=params(53.75),
        name="head",
    )(parts, long_filter)
    halo = lax.ppermute(last, "seq", [(i, i + 1) for i in range(nseq - 1)])
    group = lax.axis_index("grp")

    def from_shift(x, shift):
        return lax.ppermute(x, "grp", [((i + shift) % ngrp, i) for i in range(ngrp)])

    two = jnp.concatenate([own, from_shift(own, 4)], axis=0)
    block = 1024
    z = pl.pallas_call(
        gate_kernel,
        out_shape=jax.ShapeDtypeStruct((nseq, half, 2 * chans), BF16),
        in_specs=[pl.BlockSpec(memory_space=pltpu.SMEM), hbm] + vmem(1) + [hbm],
        out_specs=hbm,
        scratch_shapes=[
            pltpu.VMEM((2, tok, width), BF16),
            pltpu.VMEM(short_weight.shape, F32),
            pltpu.VMEM((nseq, half, 2 * chans), BF16),
            pltpu.SemaphoreType.DMA((5,)),
            pltpu.SemaphoreType.DMA((4,)),
        ],
        compiler_params=params(53.75),
        cost_estimate=pl.CostEstimate(flops=1000000000, bytes_accessed=2000000, transcendentals=0),
        name="gate",
    )(alive, parts, halo, short_weight)
    z, two = lax.optimization_barrier((z, two))
    across = [((i + (2 if i % 2 == 0 else 6)) % ngrp, i) for i in range(ngrp)]
    others = [lax.ppermute(two, "grp", across), from_shift(two, 1), from_shift(two, 7)]
    z = lax.all_to_all(z, "seq", split_axis=0, concat_axis=0, tiled=True)

    query = pl.pallas_call(
        query_kernel,
        grid=(width // block,),
        out_shape=jax.ShapeDtypeStruct((tok, width), F32),
        in_specs=[
            pl.BlockSpec(memory_space=pltpu.SMEM),
            pl.BlockSpec((1, tok, block), lambda i: (0, 0, i)),
            pl.BlockSpec((1, 2, block), lambda i: (0, 0, i)),
            pl.BlockSpec((1, 3, block), lambda i: (0, 0, i)),
        ],
        out_specs=pl.BlockSpec((tok, block), lambda i: (0, i)),
        compiler_params=params(48),
        cost_estimate=pl.CostEstimate(flops=2000000, bytes_accessed=2000000, transcendentals=0),
        name="query",
    )(alive, parts, halo, short_weight)

    table_scratch = [
        pltpu.VMEM((nseq // 2, 2 * tok, 2 * chans), F32),
        pltpu.VMEM(mats.shape, BF16),
        pltpu.VMEM(turns.shape, F32),
    ]
    y = pl.pallas_call(
        conv_kernel,
        out_shape=jax.ShapeDtypeStruct((nseq, half, 2 * chans), BF16),
        in_specs=[pl.BlockSpec(memory_space=pltpu.SMEM)] + vmem(6) + [hbm] * 2,
        out_specs=hbm,
        scratch_shapes=[
            pltpu.VMEM((nseq, half, 2 * chans), BF16),
            pltpu.VMEM((nseq * (half + PAD), 128), F32),
            pltpu.VMEM((half * (2 * nseq + PAD), 128), F32),
            pltpu.VMEM((nseq * (half + PAD), 128), F32),
            pltpu.VMEM((half * (2 * nseq + PAD), 128), F32),
            pltpu.VMEM((nseq // 2 * (2 * tok + PAD), 128), F32),
            *table_scratch,
            pltpu.SemaphoreType.DMA((4,)),
        ],
        compiler_params=params(52),
        name="convolve",
    )(group[None], two, *others, filter_bias[None], z, mats, turns)
    y = lax.all_to_all(y, "seq", split_axis=0, concat_axis=0, tiled=True)

    out = pl.pallas_call(
        mix_kernel,
        out_shape=jax.ShapeDtypeStruct((tok, width), BF16),
        in_specs=vmem(2),
        out_specs=hbm,
        scratch_shapes=[
            pltpu.VMEM((tok, width), BF16),
            pltpu.SemaphoreType.DMA((4,)),
        ],
        compiler_params=params(24),
        name="mix",
    )(y, query)
    return out[None]


def solution(mesh):
    in_specs = (P("grp", "seq", None, None), P("grp"), P(), P("seq", "grp"), P("seq"))
    out_specs = P("grp", "seq", None)
    return jax.shard_map(
        per_device, mesh=mesh, in_specs=in_specs, out_specs=out_specs, check_vma=False
    )
```
